32 devices in a mesh: row: 4 (over y, x), col: 8 (over z, core).
Axes of the slice: x: 2, y: 2, z: 4, core: 2. Of those that a mesh axis runs over, the one named last changes fastest.
Arguments:
- i_list: int32 [2], replicated, may hold values from 0 to 127
- pairs: int32 [2, 2], replicated, may hold values from 0 to 127
- vir_offsets: int32 [2], replicated, may hold values from 0 to 1008, as said below
- occ_energy: float32 [128], replicated, may hold values from -2 to -0.5
- vir_energy: float32 [1024], replicated, may hold values from 0.5 to 5
- amplitudes: bfloat16 [2, 1024, 1024], P(None, 'row', 'col'), may hold values from -4 to 4
- integrals: bfloat16 [2, 1024, 16, 128], P(None, 'row', 'col'), may hold values from -1.25 to 1.25
Outputs:
- density: bfloat16 [2, 1024, 16, 128], P(None, 'row', 'col')
- amp_grad: bfloat16 [2, 1024, 1024], P(None, 'row', 'col')
The draws below stay inside these ranges and needn't reach their ends.
Inputs may be any that keep to these rules, and one draw needn't show every extreme that they name: `vir_offsets`: the first entry is a multiple of 128 and at most 896; the second is at most 1008.
All inputs are finite; a program needn't handle non-finite values.
Results may differ from the reference program's by a relative error of at most 0.012.
Values may be sent and summed in bfloat16 or wider, within the bound.
No kernel may reach another device: no remote copies, remote signals or barrier semaphores. Data moves between devices by JAX's collectives and lax.ppermute only.
A program may use at most 64 MiB of HBM per device.

```python
import jax
import jax.numpy as jnp
from jax import lax

NOCC = 128
V = 1024
NA = 128
NI = 2
NPAIR = 2
NB = 16


def draw_vir_offsets(key, part):
    key_a = jax.random.fold_in(key, 11)
    key_b = jax.random.fold_in(key, 23)
    if NA <= NB:
        start_a = jnp.full((1,), V - NA, jnp.int32)
        start_b = jax.random.randint(key_b, (1,), 0, V - NB + 1)
    else:
        start_a = jax.random.randint(key_a, (1,), 0, V // NA) * NA
        start_b = jnp.full((1,), V - NB, jnp.int32)
    return jnp.concatenate([start_a.astype(jnp.int32), start_b.astype(jnp.int32)]).astype(jnp.int32)


def with_ends(entries, stream_key, least, top_value):
    longest = entries.shape.index(max(entries.shape))
    spots = []
    for shift in (0, 1):
        where = [jax.random.randint(jax.random.fold_in(stream_key, axis), (), 0, length) for axis, length in enumerate(entries.shape)]
        where[longest] = (where[longest] + shift) % entries.shape[longest]
        spots.append(tuple(where))
    return entries.at[spots[0]].set(least).at[spots[1]].set(top_value)


def strengthened(entries, rng, source, target, blocks, factor):
    owner, partner = [(jnp.arange(entries.shape[axis_at]) // (entries.shape[axis_at] // blocks)).reshape([-1 if axis == axis_at else 1 for axis in range(entries.ndim)]) for axis_at in (source, target)]
    chosen = jax.random.permutation(rng, blocks)[partner]
    strong = (owner == chosen) | (owner == (partner + blocks // 2) % blocks)
    return jnp.where(strong, factor * entries, entries)


def steps_of(own_key, shape, cuts, least, high):
    loudness = 1.0
    for position, parts in cuts:
        heights = jax.random.uniform(jax.random.fold_in(jax.random.fold_in(own_key, 6), position), (parts,), jnp.float32, least / len(cuts), high / len(cuts))
        loudness = loudness * jnp.repeat(jnp.exp(heights), shape[position] // parts).reshape((-1,) + (1,) * (len(shape) - 1 - position))
    return loudness


def noise_with(rng, extent, scale, reach, shards, heavy, kind=jnp.bfloat16):
    drawn = scale * jax.random.normal(rng, extent, jnp.float32)
    if shards:
        drawn = drawn * steps_of(rng, extent, shards, -0.22, 0.18)
    return jnp.clip(strengthened(drawn, jax.random.fold_in(rng, 3), *heavy), -reach, reach).astype(kind)


def setup_inputs(seed: int = 0) -> dict:
    streams_of = jax.random.split(jax.random.key(seed), 8)
    return {
        "i_list": jax.random.randint(streams_of[0], (NI,), 0, NOCC).astype(jnp.int32),
        "pairs": with_ends(jax.random.randint(streams_of[1], (NPAIR, 2), 0, NOCC), jax.random.fold_in(streams_of[1], 1), 0, NOCC - 1).astype(jnp.int32),
        "vir_offsets": draw_vir_offsets(jax.random.fold_in(streams_of[7], 71), 0),
        "occ_energy": jnp.clip(jax.random.uniform(streams_of[3], (NOCC,), jnp.float32, -2.0, -0.5), -2.0, -0.5),
        "vir_energy": jnp.clip(jax.random.uniform(streams_of[4], (V,), jnp.float32, 0.5, 5.0), 0.5, 5.0),
        "amplitudes": noise_with(streams_of[5], (NPAIR, V, V), 0.2, 4.0, ((1, 4), (2, 8)), (1, 2, 8, 2.0)),
        "integrals": noise_with(streams_of[6], (NI, V, NB, NA), 0.06, 1.25, ((1, 4), (2, 8)), (2, 1, 8, 2.0)),
    }


def reference(i_list, pairs, vir_offsets, occ_energy, vir_energy, amplitudes, integrals):
    e_a = lax.dynamic_slice(vir_energy, (vir_offsets[0].astype(jnp.int32),), (NA,))
    e_b = lax.dynamic_slice(vir_energy, (vir_offsets[1].astype(jnp.int32),), (NB,))
    occ_sum = occ_energy[i_list][:, None] + occ_energy[pairs[:, 0]][None, :] + occ_energy[pairs[:, 1]][None, :]
    base = -(vir_energy[:, None, None] + e_b[None, :, None] + e_a[None, None, :]).reshape(V, NB * NA)
    densities = []
    grad_total = jnp.zeros((NPAIR, V, V), jnp.float32)
    for ii in range(NI):
        ints = integrals[ii].reshape(V, NB * NA)
        total = jnp.zeros((V, NB * NA), jnp.float32)
        grads = []
        for pp in range(NPAIR):
            triples = jnp.dot(amplitudes[pp], ints, preferred_element_type=jnp.float32)
            scaled = (triples / (occ_sum[ii, pp] + base)).astype(jnp.bfloat16)
            total = total + lax.dot_general(amplitudes[pp], scaled, (((0,), (0,)), ((), ())), preferred_element_type=jnp.float32)
            grads.append(lax.dot_general(scaled, ints, (((1,), (1,)), ((), ())), preferred_element_type=jnp.float32))
        grad_total = grad_total + jnp.stack(grads)
        densities.append(total.astype(jnp.bfloat16).reshape(V, NB, NA))
    density = jnp.stack(densities)
    return density, grad_total.astype(jnp.bfloat16)
```

```python
import functools

import jax
import jax.numpy as jnp
from jax import lax
from jax.experimental import pallas as pl
from jax.experimental.pallas import tpu as pltpu
from jax.sharding import PartitionSpec as P

CORES = 2
LANES = 128


def pick_energy(index_values, energies):
    table = jnp.arange(energies.shape[0], dtype=jnp.int32)
    onehot = (index_values[..., None] == table).astype(jnp.float32)
    return jnp.sum(onehot * energies, axis=-1)


def gathered(i_list, pairs, vir_offsets, occ_energy, vir_energy, amplitudes, integrals):
    n_pair = amplitudes.shape[0]
    block_c = amplitudes.shape[1]
    width = vir_energy.shape[0]
    n_i = integrals.shape[0]
    block_d = integrals.shape[1]
    width_b = integrals.shape[2]
    width_a = integrals.shape[3]
    tile = width_b * width_a
    row_pos = lax.axis_index("row")
    col_pos = lax.axis_index("col")
    amp_full = lax.all_gather(amplitudes, "col", axis=2, tiled=True)
    amp_rows = amp_full.reshape(n_pair * block_c, width)
    occ_sum = (
        pick_energy(i_list, occ_energy)[:, None]
        + pick_energy(pairs[:, 0], occ_energy)[None, :]
        + pick_energy(pairs[:, 1], occ_energy)[None, :]
    )
    e_c = lax.dynamic_slice_in_dim(vir_energy, row_pos * block_c, block_c)
    e_b = lax.dynamic_slice_in_dim(vir_energy, vir_offsets[1] + col_pos * width_b, width_b)
    e_a = lax.dynamic_slice_in_dim(vir_energy, vir_offsets[0], width_a)
    base = -(e_c[:, None, None] + e_b[None, :, None] + e_a[None, None, :]).reshape(block_c, tile)
    grad_sum = jnp.zeros((n_pair, block_c, width), jnp.float32)
    dens_list = []
    for slot in range(n_i):
        ints_full = lax.all_gather(integrals[slot], "row", axis=0, tiled=True).reshape(width, tile)
        triples = jnp.einsum("pcd,dx->pcx", amp_full, ints_full, preferred_element_type=jnp.float32)
        scaled = (triples / (occ_sum[slot][:, None, None] + base[None])).astype(jnp.bfloat16)
        z_rows = scaled.reshape(n_pair * block_c, tile)
        dens_part = lax.psum_scatter(
            lax.dot_general(
                amp_rows, z_rows, (((0,), (0,)), ((), ())), preferred_element_type=jnp.float32
            ).astype(jnp.bfloat16),
            "row",
            scatter_dimension=0,
            tiled=True,
        )
        dens_list.append(dens_part.reshape(block_d, width_b, width_a))
        grad_sum = grad_sum + jnp.einsum(
            "pcx,dx->pcd", scaled, ints_full, preferred_element_type=jnp.float32
        )
    density = jnp.stack(dens_list)
    amp_grad = lax.psum_scatter(grad_sum, "col", scatter_dimension=2, tiled=True).astype(
        jnp.bfloat16
    )
    return (density, amp_grad)


def products(n_row, n_chip, *refs):
    refs = list(refs)
    i_list, pairs, vir_offsets, occ_energy, vir_smem, vir_rows = refs[:6]
    mine = refs[6 : 6 + n_chip]
    other = refs[6 + n_chip : 6 + 2 * n_chip]
    ints = refs[6 + 2 * n_chip : 6 + 2 * n_chip + n_row]
    outs = refs[6 + 2 * n_chip + n_row :]
    dens_out = outs[:n_row]
    grad_mine, grad_other, amp_full, ints_full = outs[n_row:]
    n_pair, block_c, width = amp_full.shape
    n_i, _, tile = ints_full.shape
    sub_d = mine[0].shape[2]
    block_d = ints[0].shape[1]
    width_b = tile // LANES
    row_pos = lax.axis_index("row")
    col_pos = lax.axis_index("col")
    chip_pos = col_pos // CORES
    core_pos = col_pos % CORES
    for step in range(n_chip):
        base_d = (chip_pos ^ step) * (CORES * sub_d)
        at_mine = pl.multiple_of(base_d + core_pos * sub_d, sub_d)
        at_other = pl.multiple_of(base_d + (1 - core_pos) * sub_d, sub_d)
        amp_full[:, :, pl.ds(at_mine, sub_d)] = mine[step][...]
        amp_full[:, :, pl.ds(at_other, sub_d)] = other[step][...]
    for step in range(n_row):
        at = pl.multiple_of((row_pos ^ step) * block_d, block_d)
        ints_full[:, pl.ds(at, block_d), :] = ints[step][...]

    rows_c = block_c // LANES
    e_c = vir_rows[pl.ds(row_pos * rows_c, rows_c), :]
    e_c = jnp.concatenate(
        [jnp.broadcast_to(e_c[k : k + 1, :], (LANES, LANES)).T for k in range(rows_c)], axis=0
    )
    e_a = vir_rows[pl.ds(vir_offsets[0] // LANES, 1), :]
    base = []
    for b in range(width_b):
        e_b = vir_smem[vir_offsets[1] + col_pos * width_b + b]
        base.append(-((e_c + e_b) + e_a))
    base = jnp.concatenate(base, axis=1)

    scaled = []
    for slot in range(n_i):
        for pair in range(n_pair):
            occ = (
                occ_energy[i_list[slot]]
                + occ_energy[pairs[pair, 0]]
                + occ_energy[pairs[pair, 1]]
            )
            triples = jnp.dot(amp_full[pair], ints_full[slot], preferred_element_type=jnp.float32)
            scaled.append((triples / (occ + base)).astype(jnp.bfloat16))

    for step in range(n_chip):
        base_d = (chip_pos ^ step) * (CORES * sub_d)
        for core, out in ((core_pos, grad_mine), (1 - core_pos, grad_other)):
            at = pl.multiple_of(base_d + core * sub_d, sub_d)
            for pair in range(n_pair):
                total = None
                for slot in range(n_i):
                    part = lax.dot_general(
                        scaled[slot * n_pair + pair],
                        ints_full[slot, pl.ds(at, sub_d), :],
                        (((1,), (1,)), ((), ())),
                        preferred_element_type=jnp.float32,
                    )
                    total = part if total is None else total + part
                out[step, pair] = total.astype(out.dtype)

    for step in range(n_row):
        at = pl.multiple_of((row_pos ^ step) * block_d, block_d)
        for slot in range(n_i):
            total = None
            for pair in range(n_pair):
                part = lax.dot_general(
                    amp_full[pair, :, pl.ds(at, block_d)],
                    scaled[slot * n_pair + pair],
                    (((0,), (0,)), ((), ())),
                    preferred_element_type=jnp.float32,
                )
                total = part if total is None else total + part
            dens_out[step][slot] = total.astype(dens_out[step].dtype)


def core_sums(n_chip, own, received, kept, *outs):
    kept[...] = own[0] + received[0].astype(jnp.float32)
    for step in range(1, n_chip):
        total = own[step] + received[step].astype(jnp.float32)
        outs[step - 1][...] = total.astype(outs[step - 1].dtype)


def exchanged(n_row, n_col, *args):
    i_list, pairs, vir_offsets, occ_energy, vir_energy, amplitudes, integrals = args
    n_pair, block_c, sub_d = amplitudes.shape
    n_i, block_d, width_b, width_a = integrals.shape
    width = vir_energy.shape[0]
    tile = width_b * width_a
    n_chip = n_col // CORES

    def over_row(value, mask):
        return lax.ppermute(value, "row", [(k, k ^ mask) for k in range(n_row)])

    def over_chips(value, mask):
        return lax.ppermute(value, "col", [(k, k ^ (CORES * mask)) for k in range(n_col)])

    def over_cores(value):
        return lax.ppermute(value, "col", [(k, k ^ 1) for k in range(n_col)])

    ints_own = integrals.reshape(n_i, block_d, tile)
    mine = [amplitudes] + [over_chips(amplitudes, step) for step in range(1, n_chip)]
    ints = [ints_own] + [over_row(ints_own, step) for step in range(1, n_row)]
    other = [over_cores(value) for value in mine]

    vmem = pl.BlockSpec(memory_space=pltpu.VMEM)
    smem = pl.BlockSpec(memory_space=pltpu.SMEM)
    f32, bf16 = jnp.float32, jnp.bfloat16
    flops = 6 * n_i * n_pair * block_c * width * tile
    results = pl.pallas_call(
        functools.partial(products, n_row, n_chip),
        out_shape=[
            jax.ShapeDtypeStruct((n_i, block_d, tile), f32 if step == 0 else bf16)
            for step in range(n_row)
        ]
        + [
            jax.ShapeDtypeStruct((n_chip, n_pair, block_c, sub_d), f32),
            jax.ShapeDtypeStruct((n_chip, n_pair, block_c, sub_d), bf16),
        ],
        in_specs=[smem] * 5 + [vmem] * (1 + 2 * n_chip + n_row),
        out_specs=[vmem] * (n_row + 2),
        scratch_shapes=[
            pltpu.VMEM((n_pair, block_c, width), bf16),
            pltpu.VMEM((n_i, width, tile), bf16),
        ],
        compiler_params=pltpu.CompilerParams(vmem_limit_bytes=40 * 2**20),
        cost_estimate=pl.CostEstimate(flops=flops, bytes_accessed=8 * 2**20, transcendentals=0),
        name="products",
    )(
        i_list,
        pairs,
        vir_offsets,
        occ_energy,
        vir_energy,
        vir_energy.reshape(width // LANES, LANES),
        *mine,
        *other,
        *ints,
    )
    dens = results[:n_row]
    grad_mine, grad_other = results[n_row:]
    block = (n_pair, block_c, sub_d)
    grads = pl.pallas_call(
        functools.partial(core_sums, n_chip),
        out_shape=[
            jax.ShapeDtypeStruct(block, f32 if step == 0 else bf16) for step in range(n_chip)
        ],
        in_specs=[vmem] * 2,
        out_specs=[vmem] * n_chip,
        compiler_params=pltpu.CompilerParams(vmem_limit_bytes=24 * 2**20),
        name="core_sums",
    )(grad_mine, over_cores(grad_other))
    dens_in = [over_row(dens[step], step) for step in range(1, n_row)]
    grad_in = [over_chips(grads[step], step) for step in range(1, n_chip)]
    density = dens[0]
    for value in dens_in:
        density = density + value.astype(f32)
    amp_grad = grads[0]
    for value in grad_in:
        amp_grad = amp_grad + value.astype(f32)
    return (
        density.astype(bf16).reshape(n_i, block_d, width_b, width_a),
        amp_grad.astype(bf16),
    )


def solution(mesh):
    n_row, n_col = mesh.shape["row"], mesh.shape["col"]

    def local(*args):
        block_c, sub_d = args[5].shape[1:]
        block_d, _, width_a = args[6].shape[1:]
        whole_tiles = (
            width_a == LANES
            and sub_d % LANES == 0
            and block_c % LANES == 0
            and block_d % LANES == 0
            and n_row & (n_row - 1) == 0
            and n_col & (n_col - 1) == 0
        )
        if whole_tiles:
            return exchanged(n_row, n_col, *args)
        return gathered(*args)

    return jax.shard_map(
        local,
        mesh=mesh,
        in_specs=(P(), P(), P(), P(), P(), P(None, "row", "col"), P(None, "row", "col", None)),
        out_specs=(P(None, "row", "col", None), P(None, "row", "col")),
        check_vma=False,
    )
```

```python
import functools

import jax
import jax.numpy as jnp
from jax import lax
from jax.experimental import pallas as pl
from jax.experimental.pallas import tpu as pltpu
from jax.sharding import PartitionSpec as P

CORES = 2
LANES = 128


def pick_energy(index_values, energies):
    table = jnp.arange(energies.shape[0], dtype=jnp.int32)
    onehot = (index_values[..., None] == table).astype(jnp.float32)
    return jnp.sum(onehot * energies, axis=-1)


def gathered(i_list, pairs, vir_offsets, occ_energy, vir_energy, amplitudes, integrals):
    n_pair = amplitudes.shape[0]
    block_c = amplitudes.shape[1]
    width = vir_energy.shape[0]
    n_i = integrals.shape[0]
    block_d = integrals.shape[1]
    width_b = integrals.shape[2]
    width_a = integrals.shape[3]
    tile = width_b * width_a
    row_pos = lax.axis_index("row")
    col_pos = lax.axis_index("col")
    amp_full = lax.all_gather(amplitudes, "col", axis=2, tiled=True)
    amp_rows = amp_full.reshape(n_pair * block_c, width)
    occ_sum = (
        pick_energy(i_list, occ_energy)[:, None]
        + pick_energy(pairs[:, 0], occ_energy)[None, :]
        + pick_energy(pairs[:, 1], occ_energy)[None, :]
    )
    e_c = lax.dynamic_slice_in_dim(vir_energy, row_pos * block_c, block_c)
    e_b = lax.dynamic_slice_in_dim(vir_energy, vir_offsets[1] + col_pos * width_b, width_b)
    e_a = lax.dynamic_slice_in_dim(vir_energy, vir_offsets[0], width_a)
    base = -(e_c[:, None, None] + e_b[None, :, None] + e_a[None, None, :]).reshape(block_c, tile)
    grad_sum = jnp.zeros((n_pair, block_c, width), jnp.float32)
    dens_list = []
    for slot in range(n_i):
        ints_full = lax.all_gather(integrals[slot], "row", axis=0, tiled=True).reshape(width, tile)
        triples = jnp.einsum("pcd,dx->pcx", amp_full, ints_full, preferred_element_type=jnp.float32)
        scaled = (triples / (occ_sum[slot][:, None, None] + base[None])).astype(jnp.bfloat16)
        z_rows = scaled.reshape(n_pair * block_c, tile)
        dens_part = lax.psum_scatter(
            lax.dot_general(
                amp_rows, z_rows, (((0,), (0,)), ((), ())), preferred_element_type=jnp.float32
            ).astype(jnp.bfloat16),
            "row",
            scatter_dimension=0,
            tiled=True,
        )
        dens_list.append(dens_part.reshape(block_d, width_b, width_a))
        grad_sum = grad_sum + jnp.einsum(
            "pcx,dx->pcd", scaled, ints_full, preferred_element_type=jnp.float32
        )
    density = jnp.stack(dens_list)
    amp_grad = lax.psum_scatter(grad_sum, "col", scatter_dimension=2, tiled=True).astype(
        jnp.bfloat16
    )
    return (density, amp_grad)


def products(n_row, n_chip, *refs):
    refs = list(refs)
    i_list, pairs, vir_offsets, occ_energy, vir_smem, vir_rows = refs[:6]
    mine = refs[6 : 6 + n_chip]
    other = refs[6 + n_chip : 6 + 2 * n_chip]
    ints = refs[6 + 2 * n_chip : 6 + 2 * n_chip + n_row]
    outs = refs[6 + 2 * n_chip + n_row :]
    dens_out = outs[:n_row]
    grad_mine, grad_other, amp_full, ints_full = outs[n_row:]
    n_pair, block_c, width = amp_full.shape
    n_i, _, tile = ints_full.shape
    sub_d = mine[0].shape[2]
    block_d = ints[0].shape[1]
    width_b = tile // LANES
    row_pos = lax.axis_index("row")
    col_pos = lax.axis_index("col")
    chip_pos = col_pos // CORES
    core_pos = col_pos % CORES
    for step in range(n_chip):
        base_d = (chip_pos ^ step) * (CORES * sub_d)
        at_mine = pl.multiple_of(base_d + core_pos * sub_d, sub_d)
        at_other = pl.multiple_of(base_d + (1 - core_pos) * sub_d, sub_d)
        amp_full[:, :, pl.ds(at_mine, sub_d)] = mine[step][...]
        amp_full[:, :, pl.ds(at_other, sub_d)] = other[step][...]
    for step in range(n_row):
        at = pl.multiple_of((row_pos ^ step) * block_d, block_d)
        ints_full[:, pl.ds(at, block_d), :] = ints[step][...]

    rows_c = block_c // LANES
    e_c = vir_rows[pl.ds(row_pos * rows_c, rows_c), :]
    e_c = jnp.concatenate(
        [jnp.broadcast_to(e_c[k : k + 1, :], (LANES, LANES)).T for k in range(rows_c)], axis=0
    )
    e_a = vir_rows[pl.ds(vir_offsets[0] // LANES, 1), :]
    base = []
    for b in range(width_b):
        e_b = vir_smem[vir_offsets[1] + col_pos * width_b + b]
        base.append(-((e_c + e_b) + e_a))
    base = jnp.concatenate(base, axis=1)

    scaled = []
    for slot in range(n_i):
        for pair in range(n_pair):
            occ = (
                occ_energy[i_list[slot]]
                + occ_energy[pairs[pair, 0]]
                + occ_energy[pairs[pair, 1]]
            )
            triples = jnp.dot(amp_full[pair], ints_full[slot], preferred_element_type=jnp.float32)
            scaled.append((triples / (occ + base)).astype(jnp.bfloat16))

    low = core_pos == 0
    for step in range(n_chip):
        at = pl.multiple_of((chip_pos ^ step) * (CORES * sub_d), CORES * sub_d)
        for pair in range(n_pair):
            total = None
            for slot in range(n_i):
                part = lax.dot_general(
                    scaled[slot * n_pair + pair],
                    ints_full[slot, pl.ds(at, CORES * sub_d), :],
                    (((1,), (1,)), ((), ())),
                    preferred_element_type=jnp.float32,
                )
                total = part if total is None else total + part
            first, second = total[:, :sub_d], total[:, sub_d:]
            grad_mine[step, pair] = jnp.where(low, first, second).astype(grad_mine.dtype)
            grad_other[step, pair] = jnp.where(low, second, first).astype(grad_other.dtype)

    for step in range(n_row):
        at = pl.multiple_of((row_pos ^ step) * block_d, block_d)
        for slot in range(n_i):
            total = None
            for pair in range(n_pair):
                part = lax.dot_general(
                    amp_full[pair, :, pl.ds(at, block_d)],
                    scaled[slot * n_pair + pair],
                    (((0,), (0,)), ((), ())),
                    preferred_element_type=jnp.float32,
                )
                total = part if total is None else total + part
            dens_out[step][slot] = total.astype(dens_out[step].dtype)


def core_sums(n_chip, own, received, kept, *outs):
    kept[...] = own[0] + received[0].astype(jnp.float32)
    for step in range(1, n_chip):
        total = own[step] + received[step].astype(jnp.float32)
        outs[step - 1][...] = total.astype(outs[step - 1].dtype)


def exchanged(n_row, n_col, *args):
    i_list, pairs, vir_offsets, occ_energy, vir_energy, amplitudes, integrals = args
    n_pair, block_c, sub_d = amplitudes.shape
    n_i, block_d, width_b, width_a = integrals.shape
    width = vir_energy.shape[0]
    tile = width_b * width_a
    n_chip = n_col // CORES

    def over_row(value, mask):
        return lax.ppermute(value, "row", [(k, k ^ mask) for k in range(n_row)])

    def over_chips(value, mask):
        return lax.ppermute(value, "col", [(k, k ^ (CORES * mask)) for k in range(n_col)])

    def over_cores(value):
        return lax.ppermute(value, "col", [(k, k ^ 1) for k in range(n_col)])

    mine = [amplitudes] + [over_chips(amplitudes, step) for step in range(1, n_chip)]
    near = [over_row(integrals, 1), over_row(integrals, 2)]
    half = n_i // 2
    far = jnp.concatenate([over_row(near[0][:half], 2), over_row(near[1][half:], 1)])
    ints = [value.reshape(n_i, block_d, tile) for value in [integrals] + near + [far]]
    other = [over_cores(value) for value in mine]

    vmem = pl.BlockSpec(memory_space=pltpu.VMEM)
    smem = pl.BlockSpec(memory_space=pltpu.SMEM)
    f32, bf16 = jnp.float32, jnp.bfloat16
    flops = 6 * n_i * n_pair * block_c * width * tile
    results = pl.pallas_call(
        functools.partial(products, n_row, n_chip),
        out_shape=[
            jax.ShapeDtypeStruct((n_i, block_d, tile), f32 if step == 0 else bf16)
            for step in range(n_row)
        ]
        + [
            jax.ShapeDtypeStruct((n_chip, n_pair, block_c, sub_d), f32),
            jax.ShapeDtypeStruct((n_chip, n_pair, block_c, sub_d), bf16),
        ],
        in_specs=[smem] * 5 + [vmem] * (1 + 2 * n_chip + n_row),
        out_specs=[vmem] * (n_row + 2),
        scratch_shapes=[
            pltpu.VMEM((n_pair, block_c, width), bf16),
            pltpu.VMEM((n_i, width, tile), bf16),
        ],
        compiler_params=pltpu.CompilerParams(vmem_limit_bytes=40 * 2**20),
        cost_estimate=pl.CostEstimate(flops=flops, bytes_accessed=8 * 2**20, transcendentals=0),
        name="products",
    )(
        i_list,
        pairs,
        vir_offsets,
        occ_energy,
        vir_energy,
        vir_energy.reshape(width // LANES, LANES),
        *mine,
        *other,
        *ints,
    )
    dens = results[:n_row]
    grad_mine, grad_other = results[n_row:]
    block = (n_pair, block_c, sub_d)
    grads = pl.pallas_call(
        functools.partial(core_sums, n_chip),
        out_shape=[
            jax.ShapeDtypeStruct(block, f32 if step == 0 else bf16) for step in range(n_chip)
        ],
        in_specs=[vmem] * 2,
        out_specs=[vmem] * n_chip,
        compiler_params=pltpu.CompilerParams(vmem_limit_bytes=24 * 2**20),
        name="core_sums",
    )(grad_mine, over_cores(grad_other))
    dens_in = [over_row(dens[step], step) for step in range(1, n_row)]
    grad_in = [over_chips(grads[step], step) for step in range(1, n_chip)]
    density = dens[0]
    for value in dens_in:
        density = density + value.astype(f32)
    amp_grad = grads[0]
    for value in grad_in:
        amp_grad = amp_grad + value.astype(f32)
    return (
        density.astype(bf16).reshape(n_i, block_d, width_b, width_a),
        amp_grad.astype(bf16),
    )


def solution(mesh):
    n_row, n_col = mesh.shape["row"], mesh.shape["col"]

    def local(*args):
        block_c, sub_d = args[5].shape[1:]
        block_d, _, width_a = args[6].shape[1:]
        whole_tiles = (
            width_a == LANES
            and sub_d % LANES == 0
            and block_c % LANES == 0
            and block_d % LANES == 0
            and n_row == 4
            and n_col & (n_col - 1) == 0
            and args[6].shape[0] % 2 == 0
        )
        if whole_tiles:
            return exchanged(n_row, n_col, *args)
        return gathered(*args)

    return jax.shard_map(
        local,
        mesh=mesh,
        in_specs=(P(), P(), P(), P(), P(), P(None, "row", "col"), P(None, "row", "col", None)),
        out_specs=(P(None, "row", "col", None), P(None, "row", "col")),
        check_vma=False,
    )
```

```python
import functools

import jax
import jax.numpy as jnp
from jax import lax
from jax.experimental import pallas as pl
from jax.experimental.pallas import tpu as pltpu
from jax.sharding import PartitionSpec as P

CORES = 2
LANES = 128
X_MASK, Y_MASK = 1, 2


def pick_energy(index_values, energies):
    table = jnp.arange(energies.shape[0], dtype=jnp.int32)
    onehot = (index_values[..., None] == table).astype(jnp.float32)
    return jnp.sum(onehot * energies, axis=-1)


def gathered(i_list, pairs, vir_offsets, occ_energy, vir_energy, amplitudes, integrals):
    n_pair = amplitudes.shape[0]
    block_c = amplitudes.shape[1]
    width = vir_energy.shape[0]
    n_i = integrals.shape[0]
    block_d = integrals.shape[1]
    width_b = integrals.shape[2]
    width_a = integrals.shape[3]
    tile = width_b * width_a
    row_pos = lax.axis_index("row")
    col_pos = lax.axis_index("col")
    amp_full = lax.all_gather(amplitudes, "col", axis=2, tiled=True)
    amp_rows = amp_full.reshape(n_pair * block_c, width)
    occ_sum = (
        pick_energy(i_list, occ_energy)[:, None]
        + pick_energy(pairs[:, 0], occ_energy)[None, :]
        + pick_energy(pairs[:, 1], occ_energy)[None, :]
    )
    e_c = lax.dynamic_slice_in_dim(vir_energy, row_pos * block_c, block_c)
    e_b = lax.dynamic_slice_in_dim(vir_energy, vir_offsets[1] + col_pos * width_b, width_b)
    e_a = lax.dynamic_slice_in_dim(vir_energy, vir_offsets[0], width_a)
    base = -(e_c[:, None, None] + e_b[None, :, None] + e_a[None, None, :]).reshape(block_c, tile)
    grad_sum = jnp.zeros((n_pair, block_c, width), jnp.float32)
    dens_list = []
    for slot in range(n_i):
        ints_full = lax.all_gather(integrals[slot], "row", axis=0, tiled=True).reshape(width, tile)
        triples = jnp.einsum("pcd,dx->pcx", amp_full, ints_full, preferred_element_type=jnp.float32)
        scaled = (triples / (occ_sum[slot][:, None, None] + base[None])).astype(jnp.bfloat16)
        z_rows = scaled.reshape(n_pair * block_c, tile)
        dens_part = lax.psum_scatter(
            lax.dot_general(
                amp_rows, z_rows, (((0,), (0,)), ((), ())), preferred_element_type=jnp.float32
            ).astype(jnp.bfloat16),
            "row",
            scatter_dimension=0,
            tiled=True,
        )
        dens_list.append(dens_part.reshape(block_d, width_b, width_a))
        grad_sum = grad_sum + jnp.einsum(
            "pcx,dx->pcd", scaled, ints_full, preferred_element_type=jnp.float32
        )
    density = jnp.stack(dens_list)
    amp_grad = lax.psum_scatter(grad_sum, "col", scatter_dimension=2, tiled=True).astype(
        jnp.bfloat16
    )
    return (density, amp_grad)


def denominators(
    i_list, pairs, vir_offsets, occ_energy, vir_smem, vir_rows, denom
):
    n_i, n_pair, block_c, tile = denom.shape
    width_b = tile // LANES
    row_pos = lax.axis_index("row")
    col_pos = lax.axis_index("col")
    rows_c = block_c // LANES
    e_c = vir_rows[pl.ds(row_pos * rows_c, rows_c), :]
    e_c = jnp.concatenate(
        [jnp.broadcast_to(e_c[k : k + 1, :], (LANES, LANES)).T for k in range(rows_c)], axis=0
    )
    e_a = vir_rows[pl.ds(vir_offsets[0] // LANES, 1), :]
    base = []
    for b in range(width_b):
        e_b = vir_smem[vir_offsets[1] + col_pos * width_b + b]
        base.append(-((e_c + e_b) + e_a))
    base = jnp.concatenate(base, axis=1)
    for slot in range(n_i):
        for pair in range(n_pair):
            occ = (
                occ_energy[i_list[slot]]
                + occ_energy[pairs[pair, 0]]
                + occ_energy[pairs[pair, 1]]
            )
            denom[slot, pair] = occ + base


def products(n_chip, *refs):
    denom, ints_own, ints_x, ints_y, ints_xy, ints_yx = refs[:6]
    mine = refs[6 : 6 + n_chip]
    other = refs[6 + n_chip : 6 + 2 * n_chip]
    keep_x, send_x, keep_y, send_y, grad_mine, grad_other = refs[6 + 2 * n_chip : 12 + 2 * n_chip]
    amp_full, ints_full = refs[12 + 2 * n_chip :]
    n_pair, block_c, width = amp_full.shape
    n_i, _, tile = ints_full.shape
    half = n_i // 2
    sub_d = mine[0].shape[2]
    block_d = ints_own.shape[1]
    row_pos = lax.axis_index("row")
    col_pos = lax.axis_index("col")
    chip_pos = col_pos // CORES
    core_pos = col_pos % CORES
    both = X_MASK ^ Y_MASK
    for mask, block in ((0, ints_own), (X_MASK, ints_x), (Y_MASK, ints_y)):
        at = pl.multiple_of((row_pos ^ mask) * block_d, block_d)
        ints_full[:, pl.ds(at, block_d), :] = block[...]
    at = pl.multiple_of((row_pos ^ both) * block_d, block_d)
    ints_full[:half, pl.ds(at, block_d), :] = ints_xy[...]
    ints_full[half:, pl.ds(at, block_d), :] = ints_yx[...]
    for step in range(n_chip):
        base_d = (chip_pos ^ step) * (CORES * sub_d)
        at_mine = pl.multiple_of(base_d + core_pos * sub_d, sub_d)
        at_other = pl.multiple_of(base_d + (1 - core_pos) * sub_d, sub_d)
        amp_full[:, :, pl.ds(at_mine, sub_d)] = mine[step][...]
        amp_full[:, :, pl.ds(at_other, sub_d)] = other[step][...]

    scaled = []
    for slot in range(n_i):
        for pair in range(n_pair):
            triples = jnp.dot(amp_full[pair], ints_full[slot], preferred_element_type=jnp.float32)
            scaled.append((triples / denom[slot, pair]).astype(jnp.bfloat16))

    low = core_pos == 0
    for step in range(n_chip):
        at = pl.multiple_of((chip_pos ^ step) * (CORES * sub_d), CORES * sub_d)
        for pair in range(n_pair):
            total = None
            for slot in range(n_i):
                part = lax.dot_general(
                    scaled[slot * n_pair + pair],
                    ints_full[slot, pl.ds(at, CORES * sub_d), :],
                    (((1,), (1,)), ((), ())),
                    preferred_element_type=jnp.float32,
                )
                total = part if total is None else total + part
            first, second = total[:, :sub_d], total[:, sub_d:]
            grad_mine[step, pair] = jnp.where(low, first, second).astype(grad_mine.dtype)
            grad_other[step, pair] = jnp.where(low, second, first).astype(grad_other.dtype)

    plan = ((0, 0, keep_x, 0), (0, Y_MASK, keep_x, 1), (0, X_MASK, send_x, 0), (0, both, send_x, 1))
    plan += ((1, 0, keep_y, 0), (1, X_MASK, keep_y, 1), (1, Y_MASK, send_y, 0), (1, both, send_y, 1))
    for part_of, mask, out, place in plan:
        at = pl.multiple_of((row_pos ^ mask) * block_d, block_d)
        for k in range(half):
            slot = part_of * half + k
            total = None
            for pair in range(n_pair):
                part = lax.dot_general(
                    amp_full[pair, :, pl.ds(at, block_d)],
                    scaled[slot * n_pair + pair],
                    (((0,), (0,)), ((), ())),
                    preferred_element_type=jnp.float32,
                )
                total = part if total is None else total + part
            out[place, k] = total.astype(out.dtype)


def results(own_x, last_x, own_y, last_y, own, *refs):
    density, amp_grad = refs[-2:]
    total = own[...]
    for value in refs[:-2]:
        total = total + value[...].astype(jnp.float32)
    amp_grad[...] = total.astype(amp_grad.dtype)
    half = own_x.shape[0]
    for part_of, (kept, last) in enumerate(((own_x, last_x), (own_y, last_y))):
        for k in range(half):
            total = (kept[k] + last[k].astype(jnp.float32)).astype(density.dtype)
            density[part_of * half + k] = total.reshape(density.shape[1:])


def row_sums(keep, received, own, onward):
    own[...] = keep[0] + received[0].astype(jnp.float32)
    onward[...] = (keep[1] + received[1].astype(jnp.float32)).astype(onward.dtype)


def core_sums(n_chip, own, received, kept, *outs):
    kept[...] = own[0] + received[0].astype(jnp.float32)
    for step in range(1, n_chip):
        total = own[step] + received[step].astype(jnp.float32)
        outs[step - 1][...] = total.astype(outs[step - 1].dtype)


def exchanged(n_row, n_col, *args):
    i_list, pairs, vir_offsets, occ_energy, vir_energy, amplitudes, integrals = args
    n_pair, block_c, sub_d = amplitudes.shape
    n_i, block_d, width_b, width_a = integrals.shape
    width = vir_energy.shape[0]
    tile = width_b * width_a
    n_chip = n_col // CORES

    def over_row(value, mask):
        return lax.ppermute(value, "row", [(k, k ^ mask) for k in range(n_row)])

    def over_chips(value, mask):
        return lax.ppermute(value, "col", [(k, k ^ (CORES * mask)) for k in range(n_col)])

    def over_cores(value):
        return lax.ppermute(value, "col", [(k, k ^ 1) for k in range(n_col)])

    vmem = pl.BlockSpec(memory_space=pltpu.VMEM)
    smem = pl.BlockSpec(memory_space=pltpu.SMEM)
    shape = jax.ShapeDtypeStruct
    f32, bf16 = jnp.float32, jnp.bfloat16

    def room(mib):
        return pltpu.CompilerParams(vmem_limit_bytes=mib * 2**20)

    def flat(value):
        return value.reshape(value.shape[:2] + (tile,))

    half = n_i // 2
    denom = pl.pallas_call(
        denominators,
        out_shape=shape((n_i, n_pair, block_c, tile), f32),
        in_specs=[smem] * 5 + [vmem],
        out_specs=vmem,
        compiler_params=room(8),
        name="denominators",
    )(i_list, pairs, vir_offsets, occ_energy, vir_energy, vir_energy.reshape(-1, LANES))
    mine = [amplitudes] + [over_chips(amplitudes, step) for step in range(1, n_chip)]
    ints_x, ints_y = over_row(integrals, X_MASK), over_row(integrals, Y_MASK)
    ints_own = flat(integrals)
    ints_y, denom = lax.optimization_barrier((ints_y, denom))
    ints_xy, ints_yx = over_row(ints_x[:half], Y_MASK), over_row(ints_y[half:], X_MASK)
    flat_x, flat_y = flat(ints_x), flat(ints_y)
    other = [over_cores(value) for value in mine]
    dens_shape = (2, half, block_d, tile)
    grad_shape = (n_chip, n_pair, block_c, sub_d)
    keep_x, send_x, keep_y, send_y, grad_mine, grad_other = pl.pallas_call(
        functools.partial(products, n_chip),
        out_shape=[shape(dens_shape, f32), shape(dens_shape, bf16)] * 2
        + [shape(grad_shape, f32), shape(grad_shape, bf16)],
        in_specs=[vmem] * (6 + 2 * n_chip),
        out_specs=[vmem] * 6,
        scratch_shapes=[
            pltpu.VMEM((n_pair, block_c, width), bf16),
            pltpu.VMEM((n_i, width, tile), bf16),
        ],
        compiler_params=room(36),
        name="products",
    )(denom, ints_own, flat_x, flat_y, flat(ints_xy), flat(ints_yx), *mine, *other)
    block = (n_pair, block_c, sub_d)
    grads = pl.pallas_call(
        functools.partial(core_sums, n_chip),
        out_shape=[shape(block, f32 if step == 0 else bf16) for step in range(n_chip)],
        in_specs=[vmem] * 2,
        out_specs=[vmem] * n_chip,
        compiler_params=room(16),
        name="core_sums",
    )(grad_mine, over_cores(grad_other))

    def summed(keep, received):
        return pl.pallas_call(
            row_sums,
            out_shape=[shape(dens_shape[1:], f32), shape(dens_shape[1:], bf16)],
            in_specs=[vmem] * 2,
            out_specs=[vmem] * 2,
            compiler_params=room(8),
            name="row_sums",
        )(keep, received)

    from_x, from_y = over_row(send_x, X_MASK), over_row(send_y, Y_MASK)
    grad_parts = [over_chips(grads[step], step) for step in range(1, n_chip)]
    from_x, from_y, grad_parts[0] = lax.optimization_barrier((from_x, from_y, grad_parts[0]))
    own_x, onward_x = summed(keep_x, from_x)
    own_y, onward_y = summed(keep_y, from_y)
    last_x, last_y = over_row(onward_x, Y_MASK), over_row(onward_y, X_MASK)
    density, amp_grad = pl.pallas_call(
        results,
        out_shape=[shape((n_i, block_d, width_b, width_a), bf16), shape(block, bf16)],
        in_specs=[vmem] * (4 + n_chip),
        out_specs=[vmem] * 2,
        compiler_params=room(16),
        name="results",
    )(own_x, last_x, own_y, last_y, grads[0], *grad_parts)
    return density, amp_grad


def solution(mesh):
    n_row, n_col = mesh.shape["row"], mesh.shape["col"]

    def local(*args):
        block_c, sub_d = args[5].shape[1:]
        block_d, _, width_a = args[6].shape[1:]
        whole_tiles = (
            width_a == LANES
            and sub_d % LANES == 0
            and block_c % LANES == 0
            and block_d % LANES == 0
            and n_row == 4
            and n_col & (n_col - 1) == 0
            and args[6].shape[0] % 2 == 0
        )
        if whole_tiles:
            return exchanged(n_row, n_col, *args)
        return gathered(*args)

    return jax.shard_map(
        local,
        mesh=mesh,
        in_specs=(P(), P(), P(), P(), P(), P(None, "row", "col"), P(None, "row", "col", None)),
        out_specs=(P(None, "row", "col", None), P(None, "row", "col")),
        check_vma=False,
    )
```

```python
import functools

import jax
import jax.numpy as jnp
from jax import lax
from jax.experimental import pallas as pl
from jax.experimental.pallas import tpu as pltpu
from jax.sharding import PartitionSpec as P

CORES = 2
LANES = 128
X_MASK, Y_MASK = 1, 2


def pick_energy(index_values, energies):
    table = jnp.arange(energies.shape[0], dtype=jnp.int32)
    onehot = (index_values[..., None] == table).astype(jnp.float32)
    return jnp.sum(onehot * energies, axis=-1)


def gathered(i_list, pairs, vir_offsets, occ_energy, vir_energy, amplitudes, integrals):
    n_pair = amplitudes.shape[0]
    block_c = amplitudes.shape[1]
    width = vir_energy.shape[0]
    n_i = integrals.shape[0]
    block_d = integrals.shape[1]
    width_b = integrals.shape[2]
    width_a = integrals.shape[3]
    tile = width_b * width_a
    row_pos = lax.axis_index("row")
    col_pos = lax.axis_index("col")
    amp_full = lax.all_gather(amplitudes, "col", axis=2, tiled=True)
    amp_rows = amp_full.reshape(n_pair * block_c, width)
    occ_sum = (
        pick_energy(i_list, occ_energy)[:, None]
        + pick_energy(pairs[:, 0], occ_energy)[None, :]
        + pick_energy(pairs[:, 1], occ_energy)[None, :]
    )
    e_c = lax.dynamic_slice_in_dim(vir_energy, row_pos * block_c, block_c)
    e_b = lax.dynamic_slice_in_dim(vir_energy, vir_offsets[1] + col_pos * width_b, width_b)
    e_a = lax.dynamic_slice_in_dim(vir_energy, vir_offsets[0], width_a)
    base = -(e_c[:, None, None] + e_b[None, :, None] + e_a[None, None, :]).reshape(block_c, tile)
    grad_sum = jnp.zeros((n_pair, block_c, width), jnp.float32)
    dens_list = []
    for slot in range(n_i):
        ints_full = lax.all_gather(integrals[slot], "row", axis=0, tiled=True).reshape(width, tile)
        triples = jnp.einsum("pcd,dx->pcx", amp_full, ints_full, preferred_element_type=jnp.float32)
        scaled = (triples / (occ_sum[slot][:, None, None] + base[None])).astype(jnp.bfloat16)
        z_rows = scaled.reshape(n_pair * block_c, tile)
        dens_part = lax.psum_scatter(
            lax.dot_general(
                amp_rows, z_rows, (((0,), (0,)), ((), ())), preferred_element_type=jnp.float32
            ).astype(jnp.bfloat16),
            "row",
            scatter_dimension=0,
            tiled=True,
        )
        dens_list.append(dens_part.reshape(block_d, width_b, width_a))
        grad_sum = grad_sum + jnp.einsum(
            "pcx,dx->pcd", scaled, ints_full, preferred_element_type=jnp.float32
        )
    density = jnp.stack(dens_list)
    amp_grad = lax.psum_scatter(grad_sum, "col", scatter_dimension=2, tiled=True).astype(
        jnp.bfloat16
    )
    return (density, amp_grad)


def denominators(
    i_list, pairs, vir_offsets, occ_energy, vir_smem, vir_rows, denom
):
    n_i, n_pair, block_c, tile = denom.shape
    width_b = tile // LANES
    row_pos = lax.axis_index("row")
    col_pos = lax.axis_index("col")
    rows_c = block_c // LANES
    e_c = vir_rows[pl.ds(row_pos * rows_c, rows_c), :]
    e_c = jnp.concatenate(
        [jnp.broadcast_to(e_c[k : k + 1, :], (LANES, LANES)).T for k in range(rows_c)], axis=0
    )
    e_a = vir_rows[pl.ds(vir_offsets[0] // LANES, 1), :]
    base = []
    for b in range(width_b):
        e_b = vir_smem[vir_offsets[1] + col_pos * width_b + b]
        base.append(-((e_c + e_b) + e_a))
    base = jnp.concatenate(base, axis=1)
    for slot in range(n_i):
        for pair in range(n_pair):
            occ = (
                occ_energy[i_list[slot]]
                + occ_energy[pairs[pair, 0]]
                + occ_energy[pairs[pair, 1]]
            )
            denom[slot, pair] = occ + base


def all_rows(own, near_x, near_y, far_xy, far_yx, full):
    half = own.shape[0] // 2
    block_d = own.shape[1]
    row_pos = lax.axis_index("row")
    for mask, block in ((0, own), (X_MASK, near_x), (Y_MASK, near_y)):
        at = pl.multiple_of((row_pos ^ mask) * block_d, block_d)
        full[:, pl.ds(at, block_d), :] = block[...]
    at = pl.multiple_of((row_pos ^ (X_MASK ^ Y_MASK)) * block_d, block_d)
    full[:half, pl.ds(at, block_d), :] = far_xy[...]
    full[half:, pl.ds(at, block_d), :] = far_yx[...]


def products(
    denom,
    ints_full,
    near,
    across,
    far,
    other_near,
    other_across,
    other_far,
    keep_x,
    send_x,
    keep_y,
    send_y,
    grad_mine,
    grad_other,
    amp_full,
):
    n_pair, block_c, width = amp_full.shape
    n_i, _, tile = ints_full.shape
    half = n_i // 2
    n_chip, _, _, sub_d = grad_mine.shape
    block_d = keep_x.shape[2]
    row_pos = lax.axis_index("row")
    col_pos = lax.axis_index("col")
    chip_pos = col_pos // CORES
    core_pos = col_pos % CORES
    both = X_MASK ^ Y_MASK
    blocks = (
        (0, near.at[0], other_near.at[0]),
        (1, near.at[1], other_near.at[1]),
        (2, far, other_far),
        (3, across, other_across),
    )
    for step, mine, other in blocks:
        base_d = (chip_pos ^ step) * (CORES * sub_d)
        at_mine = pl.multiple_of(base_d + core_pos * sub_d, sub_d)
        at_other = pl.multiple_of(base_d + (1 - core_pos) * sub_d, sub_d)
        amp_full[:, :, pl.ds(at_mine, sub_d)] = mine[...]
        amp_full[:, :, pl.ds(at_other, sub_d)] = other[...]

    scaled = []
    for slot in range(n_i):
        for pair in range(n_pair):
            triples = jnp.dot(amp_full[pair], ints_full[slot], preferred_element_type=jnp.float32)
            scaled.append((triples / denom[slot, pair]).astype(jnp.bfloat16))

    low = core_pos == 0
    for step in range(n_chip):
        at = pl.multiple_of((chip_pos ^ step) * (CORES * sub_d), CORES * sub_d)
        for pair in range(n_pair):
            total = None
            for slot in range(n_i):
                part = lax.dot_general(
                    scaled[slot * n_pair + pair],
                    ints_full[slot, pl.ds(at, CORES * sub_d), :],
                    (((1,), (1,)), ((), ())),
                    preferred_element_type=jnp.float32,
                )
                total = part if total is None else total + part
            first, second = total[:, :sub_d], total[:, sub_d:]
            grad_mine[step, pair] = jnp.where(low, first, second).astype(grad_mine.dtype)
            grad_other[step, pair] = jnp.where(low, second, first).astype(grad_other.dtype)

    plan = ((0, 0, keep_x, 0), (0, Y_MASK, keep_x, 1), (0, X_MASK, send_x, 0), (0, both, send_x, 1))
    plan += ((1, 0, keep_y, 0), (1, X_MASK, keep_y, 1), (1, Y_MASK, send_y, 0), (1, both, send_y, 1))
    for part_of, mask, out, place in plan:
        at = pl.multiple_of((row_pos ^ mask) * block_d, block_d)
        for k in range(half):
            slot = part_of * half + k
            total = None
            for pair in range(n_pair):
                part = lax.dot_general(
                    amp_full[pair, :, pl.ds(at, block_d)],
                    scaled[slot * n_pair + pair],
                    (((0,), (0,)), ((), ())),
                    preferred_element_type=jnp.float32,
                )
                total = part if total is None else total + part
            out[place, k] = total.astype(out.dtype)


def results(own_x, last_x, own_y, last_y, own, *refs):
    density, amp_grad = refs[-2:]
    total = own[...]
    for value in refs[:-2]:
        total = total + value[...].astype(jnp.float32)
    amp_grad[...] = total.astype(amp_grad.dtype)
    half = own_x.shape[0]
    for part_of, (kept, last) in enumerate(((own_x, last_x), (own_y, last_y))):
        for k in range(half):
            total = (kept[k] + last[k].astype(jnp.float32)).astype(density.dtype)
            density[part_of * half + k] = total.reshape(density.shape[1:])


def row_sums(keep, received, own, onward):
    own[...] = keep[0] + received[0].astype(jnp.float32)
    onward[...] = (keep[1] + received[1].astype(jnp.float32)).astype(onward.dtype)


def core_sums(n_chip, own, received, kept, *outs):
    kept[...] = own[0] + received[0].astype(jnp.float32)
    for step in range(1, n_chip):
        total = own[step] + received[step].astype(jnp.float32)
        outs[step - 1][...] = total.astype(outs[step - 1].dtype)


def exchanged(n_row, n_col, *args):
    i_list, pairs, vir_offsets, occ_energy, vir_energy, amplitudes, integrals = args
    n_pair, block_c, sub_d = amplitudes.shape
    n_i, block_d, width_b, width_a = integrals.shape
    width = vir_energy.shape[0]
    tile = width_b * width_a
    n_chip = n_col // CORES

    def over_row(value, mask):
        return lax.ppermute(value, "row", [(k, k ^ mask) for k in range(n_row)])

    def over_chips(value, mask):
        return lax.ppermute(value, "col", [(k, k ^ (CORES * mask)) for k in range(n_col)])

    def over_cores(value):
        return lax.ppermute(value, "col", [(k, k ^ 1) for k in range(n_col)])

    vmem = pl.BlockSpec(memory_space=pltpu.VMEM)
    smem = pl.BlockSpec(memory_space=pltpu.SMEM)
    shape = jax.ShapeDtypeStruct
    f32, bf16 = jnp.float32, jnp.bfloat16

    def room(mib):
        return pltpu.CompilerParams(vmem_limit_bytes=mib * 2**20)

    def flat(value):
        return value.reshape(value.shape[:2] + (tile,))

    half = n_i // 2
    denom = pl.pallas_call(
        denominators,
        out_shape=shape((n_i, n_pair, block_c, tile), f32),
        in_specs=[smem] * 5 + [vmem],
        out_specs=vmem,
        compiler_params=room(4),
        name="denominators",
    )(i_list, pairs, vir_offsets, occ_energy, vir_energy, vir_energy.reshape(-1, LANES))
    across, beside, far = [over_chips(amplitudes, step) for step in (3, 1, 2)]
    ints_x, ints_y = over_row(integrals, X_MASK), over_row(integrals, Y_MASK)
    ints_own = flat(integrals)
    ints_y, denom = lax.optimization_barrier((ints_y, denom))
    ints_xy, ints_yx = over_row(ints_x[:half], Y_MASK), over_row(ints_y[half:], X_MASK)
    flat_x, flat_y = flat(ints_x), flat(ints_y)
    near = jnp.stack([amplitudes, beside])
    other_near, other_across, other_far = over_cores(near), over_cores(across), over_cores(far)
    ints_full = pl.pallas_call(
        all_rows,
        out_shape=shape((n_i, width, tile), bf16),
        in_specs=[vmem] * 5,
        out_specs=vmem,
        compiler_params=room(6),
        name="all_rows",
    )(ints_own, flat_x, flat_y, flat(ints_xy), flat(ints_yx))
    dens_shape = (2, half, block_d, tile)
    grad_shape = (n_chip, n_pair, block_c, sub_d)
    keep_x, send_x, keep_y, send_y, grad_mine, grad_other = pl.pallas_call(
        products,
        out_shape=[shape(dens_shape, f32), shape(dens_shape, bf16)] * 2
        + [shape(grad_shape, f32), shape(grad_shape, bf16)],
        in_specs=[vmem] * 8,
        out_specs=[vmem] * 6,
        scratch_shapes=[pltpu.VMEM((n_pair, block_c, width), bf16)],
        compiler_params=room(14),
        name="products",
    )(denom, ints_full, near, across, far, other_near, other_across, other_far)
    block = (n_pair, block_c, sub_d)
    grads = pl.pallas_call(
        functools.partial(core_sums, n_chip),
        out_shape=[shape(block, f32 if step == 0 else bf16) for step in range(n_chip)],
        in_specs=[vmem] * 2,
        out_specs=[vmem] * n_chip,
        compiler_params=room(6),
        name="core_sums",
    )(grad_mine, over_cores(grad_other))

    def summed(keep, received):
        return pl.pallas_call(
            row_sums,
            out_shape=[shape(dens_shape[1:], f32), shape(dens_shape[1:], bf16)],
            in_specs=[vmem] * 2,
            out_specs=[vmem] * 2,
            compiler_params=room(4),
            name="row_sums",
        )(keep, received)

    from_x, from_y = over_row(send_x, X_MASK), over_row(send_y, Y_MASK)
    grad_parts = [over_chips(grads[step], step) for step in range(1, n_chip)]
    from_x, from_y, grad_parts[0] = lax.optimization_barrier((from_x, from_y, grad_parts[0]))
    own_x, onward_x = summed(keep_x, from_x)
    own_y, onward_y = summed(keep_y, from_y)
    last_x, last_y = over_row(onward_x, Y_MASK), over_row(onward_y, X_MASK)
    density, amp_grad = pl.pallas_call(
        results,
        out_shape=[shape((n_i, block_d, width_b, width_a), bf16), shape(block, bf16)],
        in_specs=[vmem] * (4 + n_chip),
        out_specs=[vmem] * 2,
        compiler_params=room(6),
        name="results",
    )(own_x, last_x, own_y, last_y, grads[0], *grad_parts)
    return density, amp_grad


def solution(mesh):
    n_row, n_col = mesh.shape["row"], mesh.shape["col"]

    def local(*args):
        block_c, sub_d = args[5].shape[1:]
        block_d, _, width_a = args[6].shape[1:]
        whole_tiles = (
            width_a == LANES
            and sub_d % LANES == 0
            and block_c % LANES == 0
            and block_d % LANES == 0
            and (n_row, n_col) == (4, 4 * CORES)
            and args[6].shape[0] % 2 == 0
        )
        if whole_tiles:
            return exchanged(n_row, n_col, *args)
        return gathered(*args)

    return jax.shard_map(
        local,
        mesh=mesh,
        in_specs=(P(), P(), P(), P(), P(), P(None, "row", "col"), P(None, "row", "col", None)),
        out_specs=(P(None, "row", "col", None), P(None, "row", "col")),
        check_vma=False,
    )
```

```python
import functools

import jax
import jax.numpy as jnp
from jax import lax
from jax.experimental import pallas as pl
from jax.experimental.pallas import tpu as pltpu
from jax.sharding import PartitionSpec as P

CORES = 2
LANES = 128
X_MASK, Y_MASK = 1, 2


def pick_energy(index_values, energies):
    table = jnp.arange(energies.shape[0], dtype=jnp.int32)
    onehot = (index_values[..., None] == table).astype(jnp.float32)
    return jnp.sum(onehot * energies, axis=-1)


def gathered(i_list, pairs, vir_offsets, occ_energy, vir_energy, amplitudes, integrals):
    n_pair = amplitudes.shape[0]
    block_c = amplitudes.shape[1]
    width = vir_energy.shape[0]
    n_i = integrals.shape[0]
    block_d = integrals.shape[1]
    width_b = integrals.shape[2]
    width_a = integrals.shape[3]
    tile = width_b * width_a
    row_pos = lax.axis_index("row")
    col_pos = lax.axis_index("col")
    amp_full = lax.all_gather(amplitudes, "col", axis=2, tiled=True)
    amp_rows = amp_full.reshape(n_pair * block_c, width)
    occ_sum = (
        pick_energy(i_list, occ_energy)[:, None]
        + pick_energy(pairs[:, 0], occ_energy)[None, :]
        + pick_energy(pairs[:, 1], occ_energy)[None, :]
    )
    e_c = lax.dynamic_slice_in_dim(vir_energy, row_pos * block_c, block_c)
    e_b = lax.dynamic_slice_in_dim(vir_energy, vir_offsets[1] + col_pos * width_b, width_b)
    e_a = lax.dynamic_slice_in_dim(vir_energy, vir_offsets[0], width_a)
    base = -(e_c[:, None, None] + e_b[None, :, None] + e_a[None, None, :]).reshape(block_c, tile)
    grad_sum = jnp.zeros((n_pair, block_c, width), jnp.float32)
    dens_list = []
    for slot in range(n_i):
        ints_full = lax.all_gather(integrals[slot], "row", axis=0, tiled=True).reshape(width, tile)
        triples = jnp.einsum("pcd,dx->pcx", amp_full, ints_full, preferred_element_type=jnp.float32)
        scaled = (triples / (occ_sum[slot][:, None, None] + base[None])).astype(jnp.bfloat16)
        z_rows = scaled.reshape(n_pair * block_c, tile)
        dens_part = lax.psum_scatter(
            lax.dot_general(
                amp_rows, z_rows, (((0,), (0,)), ((), ())), preferred_element_type=jnp.float32
            ).astype(jnp.bfloat16),
            "row",
            scatter_dimension=0,
            tiled=True,
        )
        dens_list.append(dens_part.reshape(block_d, width_b, width_a))
        grad_sum = grad_sum + jnp.einsum(
            "pcx,dx->pcd", scaled, ints_full, preferred_element_type=jnp.float32
        )
    density = jnp.stack(dens_list)
    amp_grad = lax.psum_scatter(grad_sum, "col", scatter_dimension=2, tiled=True).astype(
        jnp.bfloat16
    )
    return (density, amp_grad)


def denominators(
    i_list, pairs, vir_offsets, occ_energy, vir_smem, vir_rows, denom
):
    n_i, n_pair = i_list.shape[0], pairs.shape[0]
    block_c = denom.shape[0] // n_pair
    tile = denom.shape[1] // n_i
    width_b = tile // LANES
    row_pos = lax.axis_index("row")
    col_pos = lax.axis_index("col")
    rows_c = block_c // LANES
    e_c = vir_rows[pl.ds(row_pos * rows_c, rows_c), :]
    e_c = jnp.concatenate(
        [jnp.broadcast_to(e_c[k : k + 1, :], (LANES, LANES)).T for k in range(rows_c)], axis=0
    )
    e_a = vir_rows[pl.ds(vir_offsets[0] // LANES, 1), :]
    base = []
    for b in range(width_b):
        e_b = vir_smem[vir_offsets[1] + col_pos * width_b + b]
        base.append(-((e_c + e_b) + e_a))
    base = jnp.concatenate(base, axis=1)
    for slot in range(n_i):
        for pair in range(n_pair):
            occ = (
                occ_energy[i_list[slot]]
                + occ_energy[pairs[pair, 0]]
                + occ_energy[pairs[pair, 1]]
            )
            rows = slice(pair * block_c, (pair + 1) * block_c)
            denom[rows, slot * tile : (slot + 1) * tile] = occ + base


def first_slots(whole, part):
    part[...] = whole[: part.shape[0]]


def last_slots(whole, part):
    part[...] = whole[part.shape[0] :]


def all_rows(own, near_x, near_y, far_xy, far_yx, full):
    n_i, block_d, tile = own.shape
    half = n_i // 2
    row_pos = lax.axis_index("row")
    for mask, blocks in (
        (0, (own,)),
        (X_MASK, (near_x,)),
        (Y_MASK, (near_y,)),
        (X_MASK ^ Y_MASK, (far_xy, far_yx)),
    ):
        at = pl.multiple_of((row_pos ^ mask) * block_d, block_d)
        for slot in range(n_i):
            block = blocks[0] if slot < half else blocks[-1]
            place = slot - half if len(blocks) > 1 and slot >= half else slot
            full[pl.ds(at, block_d), slot * tile : (slot + 1) * tile] = block[place]


def products(
    denom,
    ints_full,
    ends,
    far,
    beside,
    other_ends,
    other_far,
    other_beside,
    keep_x,
    send_x,
    keep_y,
    send_y,
    grad_mine,
    grad_other,
    amp_full,
):
    n_chip, n_pair, block_c, sub_d = grad_mine.shape
    _, half, block_d, tile = keep_x.shape
    row_pos = lax.axis_index("row")
    col_pos = lax.axis_index("col")
    chip_pos = col_pos // CORES
    core_pos = col_pos % CORES
    blocks = (
        (0, ends.at[0], other_ends.at[0]),
        (1, beside, other_beside),
        (2, far, other_far),
        (3, ends.at[1], other_ends.at[1]),
    )
    for step, mine, other in blocks:
        base_d = (chip_pos ^ step) * (CORES * sub_d)
        at_mine = pl.multiple_of(base_d + core_pos * sub_d, sub_d)
        at_other = pl.multiple_of(base_d + (1 - core_pos) * sub_d, sub_d)
        for pair in range(n_pair):
            rows = slice(pair * block_c, (pair + 1) * block_c)
            amp_full[rows, pl.ds(at_mine, sub_d)] = mine[pair]
            amp_full[rows, pl.ds(at_other, sub_d)] = other[pair]

    triples = jnp.dot(amp_full[...], ints_full[...], preferred_element_type=jnp.float32)
    scaled = (triples / denom[...]).astype(jnp.bfloat16)

    low = core_pos == 0
    for step in range(n_chip):
        at = pl.multiple_of((chip_pos ^ step) * (CORES * sub_d), CORES * sub_d)
        total = lax.dot_general(
            scaled,
            ints_full[pl.ds(at, CORES * sub_d), :],
            (((1,), (1,)), ((), ())),
            preferred_element_type=jnp.float32,
        ).reshape(n_pair, block_c, CORES * sub_d)
        first, second = total[:, :, :sub_d], total[:, :, sub_d:]
        grad_mine[step] = jnp.where(low, first, second).astype(grad_mine.dtype)
        grad_other[step] = jnp.where(low, second, first).astype(grad_other.dtype)

    both = X_MASK ^ Y_MASK
    plan = (
        (0, (keep_x, 0), (keep_y, 0)),
        (X_MASK, (send_x, 0), (keep_y, 1)),
        (Y_MASK, (keep_x, 1), (send_y, 0)),
        (both, (send_x, 1), (send_y, 1)),
    )
    for mask, first, second in plan:
        at = pl.multiple_of((row_pos ^ mask) * block_d, block_d)
        total = lax.dot_general(
            amp_full[:, pl.ds(at, block_d)],
            scaled,
            (((0,), (0,)), ((), ())),
            preferred_element_type=jnp.float32,
        )
        for part_of, (out, place) in enumerate((first, second)):
            for k in range(half):
                slot = part_of * half + k
                out[place, k] = total[:, slot * tile : (slot + 1) * tile].astype(out.dtype)


def results(own_x, last_x, own_y, last_y, own, *refs):
    density, amp_grad = refs[-2:]
    total = own[...]
    for value in refs[:-2]:
        total = total + value[...].astype(jnp.float32)
    amp_grad[...] = total.astype(amp_grad.dtype)
    half = own_x.shape[0]
    for part_of, (kept, last) in enumerate(((own_x, last_x), (own_y, last_y))):
        for k in range(half):
            total = (kept[k] + last[k].astype(jnp.float32)).astype(density.dtype)
            density[part_of * half + k] = total.reshape(density.shape[1:])


def row_sums(keep, received, own, onward):
    own[...] = keep[0] + received[0].astype(jnp.float32)
    onward[...] = (keep[1] + received[1].astype(jnp.float32)).astype(onward.dtype)


def core_sums(n_chip, own, received, kept, *outs):
    kept[...] = own[0] + received[0].astype(jnp.float32)
    for step in range(1, n_chip):
        total = own[step] + received[step].astype(jnp.float32)
        outs[step - 1][...] = total.astype(outs[step - 1].dtype)


def exchanged(n_row, n_col, *args):
    i_list, pairs, vir_offsets, occ_energy, vir_energy, amplitudes, integrals = args
    n_pair, block_c, sub_d = amplitudes.shape
    n_i, block_d, width_b, width_a = integrals.shape
    width = vir_energy.shape[0]
    tile = width_b * width_a
    n_chip = n_col // CORES

    def over_row(value, mask):
        return lax.ppermute(value, "row", [(k, k ^ mask) for k in range(n_row)])

    def over_chips(value, mask):
        return lax.ppermute(value, "col", [(k, k ^ (CORES * mask)) for k in range(n_col)])

    def over_cores(value):
        return lax.ppermute(value, "col", [(k, k ^ 1) for k in range(n_col)])

    vmem = pl.BlockSpec(memory_space=pltpu.VMEM)
    smem = pl.BlockSpec(memory_space=pltpu.SMEM)
    shape = jax.ShapeDtypeStruct
    f32, bf16 = jnp.float32, jnp.bfloat16

    def room(mib):
        return pltpu.CompilerParams(vmem_limit_bytes=mib * 2**20)

    def flat(value):
        return value.reshape(value.shape[:2] + (tile,))

    half = n_i // 2

    def part_of(kernel, whole):
        return pl.pallas_call(
            kernel,
            out_shape=shape((half, block_d, tile), bf16),
            in_specs=[vmem],
            out_specs=vmem,
            compiler_params=room(4),
            name=kernel.__name__,
        )(whole)

    denom = pl.pallas_call(
        denominators,
        out_shape=shape((n_pair * block_c, n_i * tile), f32),
        in_specs=[smem] * 5 + [vmem],
        out_specs=vmem,
        compiler_params=room(4),
        name="denominators",
    )(i_list, pairs, vir_offsets, occ_energy, vir_energy, vir_energy.reshape(-1, LANES))
    across, beside, far = [over_chips(amplitudes, step) for step in (3, 1, 2)]
    ints_x, ints_y = over_row(integrals, X_MASK), over_row(integrals, Y_MASK)
    ints_own = flat(integrals)
    flat_x, flat_y = flat(ints_x), flat(ints_y)
    ints_xy = over_row(part_of(first_slots, flat_x), Y_MASK)
    ints_yx = over_row(part_of(last_slots, flat_y), X_MASK)
    across, ints_own, denom = lax.optimization_barrier((across, ints_own, denom))
    ends = jnp.stack([amplitudes, across])
    other_ends, other_far, other_beside = over_cores(ends), over_cores(far), over_cores(beside)
    ints_full = pl.pallas_call(
        all_rows,
        out_shape=shape((width, n_i * tile), bf16),
        in_specs=[vmem] * 5,
        out_specs=vmem,
        compiler_params=room(6),
        name="all_rows",
    )(ints_own, flat_x, flat_y, ints_xy, ints_yx)
    dens_shape = (2, half, block_d, tile)
    grad_shape = (n_chip, n_pair, block_c, sub_d)
    keep_x, send_x, keep_y, send_y, grad_mine, grad_other = pl.pallas_call(
        products,
        out_shape=[shape(dens_shape, f32), shape(dens_shape, bf16)] * 2
        + [shape(grad_shape, f32), shape(grad_shape, bf16)],
        in_specs=[vmem] * 8,
        out_specs=[vmem] * 6,
        scratch_shapes=[pltpu.VMEM((n_pair * block_c, width), bf16)],
        compiler_params=room(14),
        name="products",
    )(denom, ints_full, ends, far, beside, other_ends, other_far, other_beside)
    block = (n_pair, block_c, sub_d)
    grads = pl.pallas_call(
        functools.partial(core_sums, n_chip),
        out_shape=[shape(block, f32 if step == 0 else bf16) for step in range(n_chip)],
        in_specs=[vmem] * 2,
        out_specs=[vmem] * n_chip,
        compiler_params=room(6),
        name="core_sums",
    )(grad_mine, over_cores(grad_other))

    def summed(keep, received):
        return pl.pallas_call(
            row_sums,
            out_shape=[shape(dens_shape[1:], f32), shape(dens_shape[1:], bf16)],
            in_specs=[vmem] * 2,
            out_specs=[vmem] * 2,
            compiler_params=room(4),
            name="row_sums",
        )(keep, received)

    from_x, from_y = over_row(send_x, X_MASK), over_row(send_y, Y_MASK)
    grad_parts = [over_chips(grads[step], step) for step in range(1, n_chip)]
    from_x, from_y, grad_parts[0] = lax.optimization_barrier((from_x, from_y, grad_parts[0]))
    own_x, onward_x = summed(keep_x, from_x)
    own_y, onward_y = summed(keep_y, from_y)
    last_x, last_y = over_row(onward_x, Y_MASK), over_row(onward_y, X_MASK)
    density, amp_grad = pl.pallas_call(
        results,
        out_shape=[shape((n_i, block_d, width_b, width_a), bf16), shape(block, bf16)],
        in_specs=[vmem] * (4 + n_chip),
        out_specs=[vmem] * 2,
        compiler_params=room(6),
        name="results",
    )(own_x, last_x, own_y, last_y, grads[0], *grad_parts)
    return density, amp_grad


def solution(mesh):
    n_row, n_col = mesh.shape["row"], mesh.shape["col"]

    def local(*args):
        block_c, sub_d = args[5].shape[1:]
        block_d, _, width_a = args[6].shape[1:]
        whole_tiles = (
            width_a == LANES
            and sub_d % LANES == 0
            and block_c % LANES == 0
            and block_d % LANES == 0
            and (n_row, n_col) == (4, 4 * CORES)
            and args[6].shape[0] % 2 == 0
        )
        if whole_tiles:
            return exchanged(n_row, n_col, *args)
        return gathered(*args)

    return jax.shard_map(
        local,
        mesh=mesh,
        in_specs=(P(), P(), P(), P(), P(), P(None, "row", "col"), P(None, "row", "col", None)),
        out_specs=(P(None, "row", "col", None), P(None, "row", "col")),
        check_vma=False,
    )
```

```python
import functools

import jax
import jax.numpy as jnp
from jax import lax
from jax.experimental import pallas as pl
from jax.experimental.pallas import tpu as pltpu
from jax.sharding import PartitionSpec as P

CORES = 2
LANES = 128
X_MASK, Y_MASK = 1, 2


def pick_energy(index_values, energies):
    table = jnp.arange(energies.shape[0], dtype=jnp.int32)
    onehot = (index_values[..., None] == table).astype(jnp.float32)
    return jnp.sum(onehot * energies, axis=-1)


def gathered(i_list, pairs, vir_offsets, occ_energy, vir_energy, amplitudes, integrals):
    n_pair = amplitudes.shape[0]
    block_c = amplitudes.shape[1]
    width = vir_energy.shape[0]
    n_i = integrals.shape[0]
    block_d = integrals.shape[1]
    width_b = integrals.shape[2]
    width_a = integrals.shape[3]
    tile = width_b * width_a
    row_pos = lax.axis_index("row")
    col_pos = lax.axis_index("col")
    amp_full = lax.all_gather(amplitudes, "col", axis=2, tiled=True)
    amp_rows = amp_full.reshape(n_pair * block_c, width)
    occ_sum = (
        pick_energy(i_list, occ_energy)[:, None]
        + pick_energy(pairs[:, 0], occ_energy)[None, :]
        + pick_energy(pairs[:, 1], occ_energy)[None, :]
    )
    e_c = lax.dynamic_slice_in_dim(vir_energy, row_pos * block_c, block_c)
    e_b = lax.dynamic_slice_in_dim(vir_energy, vir_offsets[1] + col_pos * width_b, width_b)
    e_a = lax.dynamic_slice_in_dim(vir_energy, vir_offsets[0], width_a)
    base = -(e_c[:, None, None] + e_b[None, :, None] + e_a[None, None, :]).reshape(block_c, tile)
    grad_sum = jnp.zeros((n_pair, block_c, width), jnp.float32)
    dens_list = []
    for slot in range(n_i):
        ints_full = lax.all_gather(integrals[slot], "row", axis=0, tiled=True).reshape(width, tile)
        triples = jnp.einsum("pcd,dx->pcx", amp_full, ints_full, preferred_element_type=jnp.float32)
        scaled = (triples / (occ_sum[slot][:, None, None] + base[None])).astype(jnp.bfloat16)
        z_rows = scaled.reshape(n_pair * block_c, tile)
        dens_part = lax.psum_scatter(
            lax.dot_general(
                amp_rows, z_rows, (((0,), (0,)), ((), ())), preferred_element_type=jnp.float32
            ).astype(jnp.bfloat16),
            "row",
            scatter_dimension=0,
            tiled=True,
        )
        dens_list.append(dens_part.reshape(block_d, width_b, width_a))
        grad_sum = grad_sum + jnp.einsum(
            "pcx,dx->pcd", scaled, ints_full, preferred_element_type=jnp.float32
        )
    density = jnp.stack(dens_list)
    amp_grad = lax.psum_scatter(grad_sum, "col", scatter_dimension=2, tiled=True).astype(
        jnp.bfloat16
    )
    return (density, amp_grad)


def denominators(
    i_list, pairs, vir_offsets, occ_energy, vir_smem, vir_rows, denom
):
    n_i, n_pair = i_list.shape[0], pairs.shape[0]
    block_c = denom.shape[0] // n_pair
    tile = denom.shape[1] // n_i
    width_b = tile // LANES
    row_pos = lax.axis_index("row")
    col_pos = lax.axis_index("col")
    rows_c = block_c // LANES
    e_c = vir_rows[pl.ds(row_pos * rows_c, rows_c), :]
    e_c = jnp.concatenate(
        [jnp.broadcast_to(e_c[k : k + 1, :], (LANES, LANES)).T for k in range(rows_c)], axis=0
    )
    e_a = vir_rows[pl.ds(vir_offsets[0] // LANES, 1), :]
    base = []
    for b in range(width_b):
        e_b = vir_smem[vir_offsets[1] + col_pos * width_b + b]
        base.append(-((e_c + e_b) + e_a))
    base = jnp.concatenate(base, axis=1)
    for slot in range(n_i):
        for pair in range(n_pair):
            occ = (
                occ_energy[i_list[slot]]
                + occ_energy[pairs[pair, 0]]
                + occ_energy[pairs[pair, 1]]
            )
            rows = slice(pair * block_c, (pair + 1) * block_c)
            denom[rows, slot * tile : (slot + 1) * tile] = occ + base


def first_slots(whole, part):
    part[...] = whole[: part.shape[0]]


def last_slots(whole, part):
    part[...] = whole[part.shape[0] :]


def all_rows(own, near_x, near_y, far_xy, far_yx, full):
    n_i, block_d, tile = own.shape
    half = n_i // 2
    row_pos = lax.axis_index("row")
    for mask, blocks in (
        (0, (own,)),
        (X_MASK, (near_x,)),
        (Y_MASK, (near_y,)),
        (X_MASK ^ Y_MASK, (far_xy, far_yx)),
    ):
        at = pl.multiple_of((row_pos ^ mask) * block_d, block_d)
        for slot in range(n_i):
            block = blocks[0] if slot < half else blocks[-1]
            place = slot - half if len(blocks) > 1 and slot >= half else slot
            full[pl.ds(at, block_d), slot * tile : (slot + 1) * tile] = block[place]


def products(
    denom,
    ints_full,
    ends,
    far,
    beside,
    other_ends,
    other_far,
    other_beside,
    keep_x,
    send_x,
    keep_y,
    send_y,
    grad_mine,
    grad_other,
    amp_full,
):
    n_chip, n_pair, block_c, sub_d = grad_mine.shape
    _, half, block_d, tile = keep_x.shape
    row_pos = lax.axis_index("row")
    col_pos = lax.axis_index("col")
    chip_pos = col_pos // CORES
    core_pos = col_pos % CORES
    blocks = (
        (0, ends.at[0], other_ends.at[0]),
        (1, beside, other_beside),
        (2, far, other_far),
        (3, ends.at[1], other_ends.at[1]),
    )
    for step, mine, other in blocks:
        base_d = (chip_pos ^ step) * (CORES * sub_d)
        at_mine = pl.multiple_of(base_d + core_pos * sub_d, sub_d)
        at_other = pl.multiple_of(base_d + (1 - core_pos) * sub_d, sub_d)
        for pair in range(n_pair):
            rows = slice(pair * block_c, (pair + 1) * block_c)
            amp_full[rows, pl.ds(at_mine, sub_d)] = mine[pair]
            amp_full[rows, pl.ds(at_other, sub_d)] = other[pair]

    triples = jnp.dot(amp_full[...], ints_full[...], preferred_element_type=jnp.float32)
    scaled = (triples / denom[...]).astype(jnp.bfloat16)

    low = core_pos == 0
    for step in range(n_chip):
        at = pl.multiple_of((chip_pos ^ step) * (CORES * sub_d), CORES * sub_d)
        total = lax.dot_general(
            scaled,
            ints_full[pl.ds(at, CORES * sub_d), :],
            (((1,), (1,)), ((), ())),
            preferred_element_type=jnp.float32,
        ).reshape(n_pair, block_c, CORES * sub_d)
        first, second = total[:, :, :sub_d], total[:, :, sub_d:]
        grad_mine[step] = jnp.where(low, first, second).astype(grad_mine.dtype)
        grad_other[step] = jnp.where(low, second, first).astype(grad_other.dtype)

    both = X_MASK ^ Y_MASK
    plan = (
        (0, (keep_x, 0), (keep_y, 0)),
        (X_MASK, (send_x, 0), (keep_y, 1)),
        (Y_MASK, (keep_x, 1), (send_y, 0)),
        (both, (send_x, 1), (send_y, 1)),
    )
    for mask, first, second in plan:
        at = pl.multiple_of((row_pos ^ mask) * block_d, block_d)
        total = lax.dot_general(
            amp_full[:, pl.ds(at, block_d)],
            scaled,
            (((0,), (0,)), ((), ())),
            preferred_element_type=jnp.float32,
        )
        for part_of, (out, place) in enumerate((first, second)):
            for k in range(half):
                slot = part_of * half + k
                out[place, k] = total[:, slot * tile : (slot + 1) * tile].astype(out.dtype)


def results(own_x, last_x, own_y, last_y, own, *refs):
    *parts, density, amp_grad, rows, block, sems = refs
    n_i = rows.shape[0]
    half = own_x.shape[0]
    copies = []
    for part_of, (kept, last) in enumerate(((own_x, last_x), (own_y, last_y))):
        for k in range(half):
            slot = part_of * half + k
            total = (kept[k] + last[k].astype(jnp.float32)).astype(rows.dtype)
            rows[slot] = total.reshape(rows.shape[1:])
            copies.append(pltpu.make_async_copy(rows.at[slot], density.at[slot], sems.at[slot]))
            copies[-1].start()
    total = own[...]
    for value in parts:
        total = total + value[...].astype(jnp.float32)
    block[...] = total.astype(block.dtype)
    copies.append(pltpu.make_async_copy(block, amp_grad, sems.at[n_i]))
    copies[-1].start()
    for copy in copies:
        copy.wait()


def row_sums(keep, received, own, onward):
    own[...] = keep[0] + received[0].astype(jnp.float32)
    onward[...] = (keep[1] + received[1].astype(jnp.float32)).astype(onward.dtype)


def core_sums(n_chip, own, received, kept, *outs):
    kept[...] = own[0] + received[0].astype(jnp.float32)
    for step in range(1, n_chip):
        total = own[step] + received[step].astype(jnp.float32)
        outs[step - 1][...] = total.astype(outs[step - 1].dtype)


def exchanged(n_row, n_col, *args):
    i_list, pairs, vir_offsets, occ_energy, vir_energy, amplitudes, integrals = args
    n_pair, block_c, sub_d = amplitudes.shape
    n_i, block_d, width_b, width_a = integrals.shape
    width = vir_energy.shape[0]
    tile = width_b * width_a
    n_chip = n_col // CORES

    def over_row(value, mask):
        return lax.ppermute(value, "row", [(k, k ^ mask) for k in range(n_row)])

    def over_chips(value, mask):
        return lax.ppermute(value, "col", [(k, k ^ (CORES * mask)) for k in range(n_col)])

    def over_cores(value):
        return lax.ppermute(value, "col", [(k, k ^ 1) for k in range(n_col)])

    vmem = pl.BlockSpec(memory_space=pltpu.VMEM)
    smem = pl.BlockSpec(memory_space=pltpu.SMEM)
    shape = jax.ShapeDtypeStruct
    f32, bf16 = jnp.float32, jnp.bfloat16

    def room(mib):
        return pltpu.CompilerParams(vmem_limit_bytes=mib * 2**20)

    def flat(value):
        return value.reshape(value.shape[:2] + (tile,))

    half = n_i // 2

    def part_of(kernel, whole):
        return pl.pallas_call(
            kernel,
            out_shape=shape((half, block_d, tile), bf16),
            in_specs=[vmem],
            out_specs=vmem,
            compiler_params=room(4),
            name=kernel.__name__,
        )(whole)

    denom = pl.pallas_call(
        denominators,
        out_shape=shape((n_pair * block_c, n_i * tile), f32),
        in_specs=[smem] * 5 + [vmem],
        out_specs=vmem,
        compiler_params=room(4),
        name="denominators",
    )(i_list, pairs, vir_offsets, occ_energy, vir_energy, vir_energy.reshape(-1, LANES))
    across, beside, far = [over_chips(amplitudes, step) for step in (3, 1, 2)]
    ints_x, ints_y = over_row(integrals, X_MASK), over_row(integrals, Y_MASK)
    ints_own = flat(integrals)
    flat_x, flat_y = flat(ints_x), flat(ints_y)
    ints_xy = over_row(part_of(first_slots, flat_x), Y_MASK)
    ints_yx = over_row(part_of(last_slots, flat_y), X_MASK)
    across, ints_own, denom = lax.optimization_barrier((across, ints_own, denom))
    ends = jnp.stack([amplitudes, across])
    other_ends, other_far, other_beside = over_cores(ends), over_cores(far), over_cores(beside)
    ints_full = pl.pallas_call(
        all_rows,
        out_shape=shape((width, n_i * tile), bf16),
        in_specs=[vmem] * 5,
        out_specs=vmem,
        compiler_params=room(6),
        name="all_rows",
    )(ints_own, flat_x, flat_y, ints_xy, ints_yx)
    dens_shape = (2, half, block_d, tile)
    grad_shape = (n_chip, n_pair, block_c, sub_d)
    keep_x, send_x, keep_y, send_y, grad_mine, grad_other = pl.pallas_call(
        products,
        out_shape=[shape(dens_shape, f32), shape(dens_shape, bf16)] * 2
        + [shape(grad_shape, f32), shape(grad_shape, bf16)],
        in_specs=[vmem] * 8,
        out_specs=[vmem] * 6,
        scratch_shapes=[pltpu.VMEM((n_pair * block_c, width), bf16)],
        compiler_params=room(14),
        name="products",
    )(denom, ints_full, ends, far, beside, other_ends, other_far, other_beside)
    block = (n_pair, block_c, sub_d)
    grads = pl.pallas_call(
        functools.partial(core_sums, n_chip),
        out_shape=[shape(block, f32 if step == 0 else bf16) for step in range(n_chip)],
        in_specs=[vmem] * 2,
        out_specs=[vmem] * n_chip,
        compiler_params=room(6),
        name="core_sums",
    )(grad_mine, over_cores(grad_other))

    def summed(keep, received):
        return pl.pallas_call(
            row_sums,
            out_shape=[shape(dens_shape[1:], f32), shape(dens_shape[1:], bf16)],
            in_specs=[vmem] * 2,
            out_specs=[vmem] * 2,
            compiler_params=room(4),
            name="row_sums",
        )(keep, received)

    from_x, from_y = over_row(send_x, X_MASK), over_row(send_y, Y_MASK)
    grad_parts = [over_chips(grads[step], step) for step in range(1, n_chip)]
    from_x, from_y, grad_parts[0] = lax.optimization_barrier((from_x, from_y, grad_parts[0]))
    own_x, onward_x = summed(keep_x, from_x)
    own_y, onward_y = summed(keep_y, from_y)
    last_x, last_y = over_row(onward_x, Y_MASK), over_row(onward_y, X_MASK)
    density, amp_grad = pl.pallas_call(
        results,
        out_shape=[shape((n_i, block_d, width_b, width_a), bf16), shape(block, bf16)],
        in_specs=[vmem] * (4 + n_chip),
        out_specs=[pl.BlockSpec(memory_space=pl.ANY)] * 2,
        scratch_shapes=[
            pltpu.VMEM((n_i, block_d, width_b, width_a), bf16),
            pltpu.VMEM(block, bf16),
            pltpu.SemaphoreType.DMA((n_i + 1,)),
        ],
        compiler_params=room(6),
        name="results",
    )(own_x, last_x, own_y, last_y, grads[0], *grad_parts)
    return density, amp_grad


def solution(mesh):
    n_row, n_col = mesh.shape["row"], mesh.shape["col"]

    def local(*args):
        block_c, sub_d = args[5].shape[1:]
        block_d, _, width_a = args[6].shape[1:]
        whole_tiles = (
            width_a == LANES
            and sub_d % LANES == 0
            and block_c % LANES == 0
            and block_d % LANES == 0
            and (n_row, n_col) == (4, 4 * CORES)
            and args[6].shape[0] % 2 == 0
        )
        if whole_tiles:
            return exchanged(n_row, n_col, *args)
        return gathered(*args)

    return jax.shard_map(
        local,
        mesh=mesh,
        in_specs=(P(), P(), P(), P(), P(), P(None, "row", "col"), P(None, "row", "col", None)),
        out_specs=(P(None, "row", "col", None), P(None, "row", "col")),
        check_vma=False,
    )
```

```python
import functools

import jax
import jax.numpy as jnp
from jax import lax
from jax.experimental import pallas as pl
from jax.experimental.pallas import tpu as pltpu
from jax.sharding import PartitionSpec as P

CORES = 2
LANES = 128
X_MASK, Y_MASK = 1, 2


def pick_energy(index_values, energies):
    table = jnp.arange(energies.shape[0], dtype=jnp.int32)
    onehot = (index_values[..., None] == table).astype(jnp.float32)
    return jnp.sum(onehot * energies, axis=-1)


def gathered(i_list, pairs, vir_offsets, occ_energy, vir_energy, amplitudes, integrals):
    n_pair = amplitudes.shape[0]
    block_c = amplitudes.shape[1]
    width = vir_energy.shape[0]
    n_i = integrals.shape[0]
    block_d = integrals.shape[1]
    width_b = integrals.shape[2]
    width_a = integrals.shape[3]
    tile = width_b * width_a
    row_pos = lax.axis_index("row")
    col_pos = lax.axis_index("col")
    amp_full = lax.all_gather(amplitudes, "col", axis=2, tiled=True)
    amp_rows = amp_full.reshape(n_pair * block_c, width)
    occ_sum = (
        pick_energy(i_list, occ_energy)[:, None]
        + pick_energy(pairs[:, 0], occ_energy)[None, :]
        + pick_energy(pairs[:, 1], occ_energy)[None, :]
    )
    e_c = lax.dynamic_slice_in_dim(vir_energy, row_pos * block_c, block_c)
    e_b = lax.dynamic_slice_in_dim(vir_energy, vir_offsets[1] + col_pos * width_b, width_b)
    e_a = lax.dynamic_slice_in_dim(vir_energy, vir_offsets[0], width_a)
    base = -(e_c[:, None, None] + e_b[None, :, None] + e_a[None, None, :]).reshape(block_c, tile)
    grad_sum = jnp.zeros((n_pair, block_c, width), jnp.float32)
    dens_list = []
    for slot in range(n_i):
        ints_full = lax.all_gather(integrals[slot], "row", axis=0, tiled=True).reshape(width, tile)
        triples = jnp.einsum("pcd,dx->pcx", amp_full, ints_full, preferred_element_type=jnp.float32)
        scaled = (triples / (occ_sum[slot][:, None, None] + base[None])).astype(jnp.bfloat16)
        z_rows = scaled.reshape(n_pair * block_c, tile)
        dens_part = lax.psum_scatter(
            lax.dot_general(
                amp_rows, z_rows, (((0,), (0,)), ((), ())), preferred_element_type=jnp.float32
            ).astype(jnp.bfloat16),
            "row",
            scatter_dimension=0,
            tiled=True,
        )
        dens_list.append(dens_part.reshape(block_d, width_b, width_a))
        grad_sum = grad_sum + jnp.einsum(
            "pcx,dx->pcd", scaled, ints_full, preferred_element_type=jnp.float32
        )
    density = jnp.stack(dens_list)
    amp_grad = lax.psum_scatter(grad_sum, "col", scatter_dimension=2, tiled=True).astype(
        jnp.bfloat16
    )
    return (density, amp_grad)


def reciprocals(
    i_list, pairs, vir_offsets, occ_energy, vir_smem, vir_rows, weights
):
    n_i, n_pair = i_list.shape[0], pairs.shape[0]
    block_c = weights.shape[0] // n_pair
    tile = weights.shape[1] // n_i
    width_b = tile // LANES
    row_pos = lax.axis_index("row")
    col_pos = lax.axis_index("col")
    rows_c = block_c // LANES
    e_c = vir_rows[pl.ds(row_pos * rows_c, rows_c), :]
    e_c = jnp.concatenate(
        [jnp.broadcast_to(e_c[k : k + 1, :], (LANES, LANES)).T for k in range(rows_c)], axis=0
    )
    e_a = vir_rows[pl.ds(vir_offsets[0] // LANES, 1), :]
    base = []
    for b in range(width_b):
        e_b = vir_smem[vir_offsets[1] + col_pos * width_b + b]
        base.append(-((e_c + e_b) + e_a))
    base = jnp.concatenate(base, axis=1)
    for slot in range(n_i):
        for pair in range(n_pair):
            occ = (
                occ_energy[i_list[slot]]
                + occ_energy[pairs[pair, 0]]
                + occ_energy[pairs[pair, 1]]
            )
            rows = slice(pair * block_c, (pair + 1) * block_c)
            weights[rows, slot * tile : (slot + 1) * tile] = 1.0 / (occ + base)


def first_slots(whole, part):
    part[...] = whole[: part.shape[0]]


def last_slots(whole, part):
    part[...] = whole[part.shape[0] :]


def all_rows(own, near_x, near_y, far_xy, far_yx, full):
    n_i, block_d, tile = own.shape
    half = n_i // 2
    row_pos = lax.axis_index("row")
    for mask, blocks in (
        (0, (own,)),
        (X_MASK, (near_x,)),
        (Y_MASK, (near_y,)),
        (X_MASK ^ Y_MASK, (far_xy, far_yx)),
    ):
        at = pl.multiple_of((row_pos ^ mask) * block_d, block_d)
        for slot in range(n_i):
            block = blocks[0] if slot < half else blocks[-1]
            place = slot - half if len(blocks) > 1 and slot >= half else slot
            full[pl.ds(at, block_d), slot * tile : (slot + 1) * tile] = block[place]


def products(
    weights,
    ints_full,
    ends,
    far,
    beside,
    other_ends,
    other_far,
    other_beside,
    keep_x,
    send_x,
    keep_y,
    send_y,
    grad_mine,
    grad_other,
    amp_full,
):
    n_chip, n_pair, block_c, sub_d = grad_mine.shape
    _, half, block_d, tile = keep_x.shape
    row_pos = lax.axis_index("row")
    col_pos = lax.axis_index("col")
    chip_pos = col_pos // CORES
    core_pos = col_pos % CORES
    blocks = (
        (0, ends.at[0], other_ends.at[0]),
        (1, beside, other_beside),
        (2, far, other_far),
        (3, ends.at[1], other_ends.at[1]),
    )
    for step, mine, other in blocks:
        base_d = (chip_pos ^ step) * (CORES * sub_d)
        at_mine = pl.multiple_of(base_d + core_pos * sub_d, sub_d)
        at_other = pl.multiple_of(base_d + (1 - core_pos) * sub_d, sub_d)
        for pair in range(n_pair):
            rows = slice(pair * block_c, (pair + 1) * block_c)
            amp_full[rows, pl.ds(at_mine, sub_d)] = mine[pair]
            amp_full[rows, pl.ds(at_other, sub_d)] = other[pair]

    triples = jnp.dot(amp_full[...], ints_full[...], preferred_element_type=jnp.float32)
    scaled = (triples * weights[...]).astype(jnp.bfloat16)

    low = core_pos == 0
    for step in range(n_chip):
        at = pl.multiple_of((chip_pos ^ step) * (CORES * sub_d), CORES * sub_d)
        total = lax.dot_general(
            scaled,
            ints_full[pl.ds(at, CORES * sub_d), :],
            (((1,), (1,)), ((), ())),
            preferred_element_type=jnp.float32,
        ).reshape(n_pair, block_c, CORES * sub_d)
        first, second = total[:, :, :sub_d], total[:, :, sub_d:]
        grad_mine[step] = jnp.where(low, first, second).astype(grad_mine.dtype)
        grad_other[step] = jnp.where(low, second, first).astype(grad_other.dtype)

    both = X_MASK ^ Y_MASK
    plan = (
        (0, (keep_x, 0), (keep_y, 0)),
        (X_MASK, (send_x, 0), (keep_y, 1)),
        (Y_MASK, (keep_x, 1), (send_y, 0)),
        (both, (send_x, 1), (send_y, 1)),
    )
    for mask, first, second in plan:
        at = pl.multiple_of((row_pos ^ mask) * block_d, block_d)
        total = lax.dot_general(
            amp_full[:, pl.ds(at, block_d)],
            scaled,
            (((0,), (0,)), ((), ())),
            preferred_element_type=jnp.float32,
        )
        for part_of, (out, place) in enumerate((first, second)):
            for k in range(half):
                slot = part_of * half + k
                out[place, k] = total[:, slot * tile : (slot + 1) * tile].astype(out.dtype)


def results(own_x, last_x, own_y, last_y, own, *refs):
    density, amp_grad = refs[-2:]
    total = own[...]
    for value in refs[:-2]:
        total = total + value[...].astype(jnp.float32)
    amp_grad[...] = total.astype(amp_grad.dtype)
    half = own_x.shape[0]
    for part_of, (kept, last) in enumerate(((own_x, last_x), (own_y, last_y))):
        for k in range(half):
            total = (kept[k] + last[k].astype(jnp.float32)).astype(density.dtype)
            density[part_of * half + k] = total.reshape(density.shape[1:])


def row_sums(keep, received, own, onward):
    own[...] = keep[0] + received[0].astype(jnp.float32)
    onward[...] = (keep[1] + received[1].astype(jnp.float32)).astype(onward.dtype)


def core_sums(n_chip, own, received, kept, *outs):
    kept[...] = own[0] + received[0].astype(jnp.float32)
    for step in range(1, n_chip):
        total = own[step] + received[step].astype(jnp.float32)
        outs[step - 1][...] = total.astype(outs[step - 1].dtype)


def exchanged(n_row, n_col, *args):
    i_list, pairs, vir_offsets, occ_energy, vir_energy, amplitudes, integrals = args
    n_pair, block_c, sub_d = amplitudes.shape
    n_i, block_d, width_b, width_a = integrals.shape
    width = vir_energy.shape[0]
    tile = width_b * width_a
    n_chip = n_col // CORES

    def over_row(value, mask):
        return lax.ppermute(value, "row", [(k, k ^ mask) for k in range(n_row)])

    def over_chips(value, mask):
        return lax.ppermute(value, "col", [(k, k ^ (CORES * mask)) for k in range(n_col)])

    def over_cores(value):
        return lax.ppermute(value, "col", [(k, k ^ 1) for k in range(n_col)])

    vmem = pl.BlockSpec(memory_space=pltpu.VMEM)
    smem = pl.BlockSpec(memory_space=pltpu.SMEM)
    shape = jax.ShapeDtypeStruct
    f32, bf16 = jnp.float32, jnp.bfloat16

    def room(mib):
        return pltpu.CompilerParams(vmem_limit_bytes=mib * 2**20)

    def flat(value):
        return value.reshape(value.shape[:2] + (tile,))

    half = n_i // 2

    def part_of(kernel, whole):
        return pl.pallas_call(
            kernel,
            out_shape=shape((half, block_d, tile), bf16),
            in_specs=[vmem],
            out_specs=vmem,
            compiler_params=room(4),
            name=kernel.__name__,
        )(whole)

    weights = pl.pallas_call(
        reciprocals,
        out_shape=shape((n_pair * block_c, n_i * tile), f32),
        in_specs=[smem] * 5 + [vmem],
        out_specs=vmem,
        compiler_params=room(4),
        name="reciprocals",
    )(i_list, pairs, vir_offsets, occ_energy, vir_energy, vir_energy.reshape(-1, LANES))
    across, beside, far = [over_chips(amplitudes, step) for step in (3, 1, 2)]
    ints_x, ints_y = over_row(integrals, X_MASK), over_row(integrals, Y_MASK)
    ints_own = flat(integrals)
    flat_x, flat_y = flat(ints_x), flat(ints_y)
    ints_xy = over_row(part_of(first_slots, flat_x), Y_MASK)
    ints_yx = over_row(part_of(last_slots, flat_y), X_MASK)
    across, ints_own, weights = lax.optimization_barrier((across, ints_own, weights))
    ends = jnp.stack([amplitudes, across])
    other_ends, other_far, other_beside = over_cores(ends), over_cores(far), over_cores(beside)
    ints_full = pl.pallas_call(
        all_rows,
        out_shape=shape((width, n_i * tile), bf16),
        in_specs=[vmem] * 5,
        out_specs=vmem,
        compiler_params=room(6),
        name="all_rows",
    )(ints_own, flat_x, flat_y, ints_xy, ints_yx)
    dens_shape = (2, half, block_d, tile)
    grad_shape = (n_chip, n_pair, block_c, sub_d)
    keep_x, send_x, keep_y, send_y, grad_mine, grad_other = pl.pallas_call(
        products,
        out_shape=[shape(dens_shape, f32), shape(dens_shape, bf16)] * 2
        + [shape(grad_shape, f32), shape(grad_shape, bf16)],
        in_specs=[vmem] * 8,
        out_specs=[vmem] * 6,
        scratch_shapes=[pltpu.VMEM((n_pair * block_c, width), bf16)],
        compiler_params=room(14),
        name="products",
    )(weights, ints_full, ends, far, beside, other_ends, other_far, other_beside)
    block = (n_pair, block_c, sub_d)
    grads = pl.pallas_call(
        functools.partial(core_sums, n_chip),
        out_shape=[shape(block, f32 if step == 0 else bf16) for step in range(n_chip)],
        in_specs=[vmem] * 2,
        out_specs=[vmem] * n_chip,
        compiler_params=room(6),
        name="core_sums",
    )(grad_mine, over_cores(grad_other))

    def summed(keep, received):
        return pl.pallas_call(
            row_sums,
            out_shape=[shape(dens_shape[1:], f32), shape(dens_shape[1:], bf16)],
            in_specs=[vmem] * 2,
            out_specs=[vmem] * 2,
            compiler_params=room(4),
            name="row_sums",
        )(keep, received)

    from_x, from_y = over_row(send_x, X_MASK), over_row(send_y, Y_MASK)
    grad_parts = [over_chips(grads[step], step) for step in range(1, n_chip)]
    from_x, from_y, grad_parts[0] = lax.optimization_barrier((from_x, from_y, grad_parts[0]))
    own_x, onward_x = summed(keep_x, from_x)
    own_y, onward_y = summed(keep_y, from_y)
    last_x, last_y = over_row(onward_x, Y_MASK), over_row(onward_y, X_MASK)
    density, amp_grad = pl.pallas_call(
        results,
        out_shape=[shape((n_i, block_d, width_b, width_a), bf16), shape(block, bf16)],
        in_specs=[vmem] * (4 + n_chip),
        out_specs=[vmem] * 2,
        compiler_params=room(6),
        name="results",
    )(own_x, last_x, own_y, last_y, grads[0], *grad_parts)
    return density, amp_grad


def solution(mesh):
    n_row, n_col = mesh.shape["row"], mesh.shape["col"]

    def local(*args):
        block_c, sub_d = args[5].shape[1:]
        block_d, _, width_a = args[6].shape[1:]
        whole_tiles = (
            width_a == LANES
            and sub_d % LANES == 0
            and block_c % LANES == 0
            and block_d % LANES == 0
            and (n_row, n_col) == (4, 4 * CORES)
            and args[6].shape[0] % 2 == 0
        )
        if whole_tiles:
            return exchanged(n_row, n_col, *args)
        return gathered(*args)

    return jax.shard_map(
        local,
        mesh=mesh,
        in_specs=(P(), P(), P(), P(), P(), P(None, "row", "col"), P(None, "row", "col", None)),
        out_specs=(P(None, "row", "col", None), P(None, "row", "col")),
        check_vma=False,
    )
```

```python
import functools

import jax
import jax.numpy as jnp
from jax import lax
from jax.experimental import pallas as pl
from jax.experimental.pallas import tpu as pltpu
from jax.sharding import PartitionSpec as P

CORES = 2
LANES = 128
X_MASK, Y_MASK = 1, 2


def pick_energy(index_values, energies):
    table = jnp.arange(energies.shape[0], dtype=jnp.int32)
    onehot = (index_values[..., None] == table).astype(jnp.float32)
    return jnp.sum(onehot * energies, axis=-1)


def gathered(i_list, pairs, vir_offsets, occ_energy, vir_energy, amplitudes, integrals):
    n_pair = amplitudes.shape[0]
    block_c = amplitudes.shape[1]
    width = vir_energy.shape[0]
    n_i = integrals.shape[0]
    block_d = integrals.shape[1]
    width_b = integrals.shape[2]
    width_a = integrals.shape[3]
    tile = width_b * width_a
    row_pos = lax.axis_index("row")
    col_pos = lax.axis_index("col")
    amp_full = lax.all_gather(amplitudes, "col", axis=2, tiled=True)
    amp_rows = amp_full.reshape(n_pair * block_c, width)
    occ_sum = (
        pick_energy(i_list, occ_energy)[:, None]
        + pick_energy(pairs[:, 0], occ_energy)[None, :]
        + pick_energy(pairs[:, 1], occ_energy)[None, :]
    )
    e_c = lax.dynamic_slice_in_dim(vir_energy, row_pos * block_c, block_c)
    e_b = lax.dynamic_slice_in_dim(vir_energy, vir_offsets[1] + col_pos * width_b, width_b)
    e_a = lax.dynamic_slice_in_dim(vir_energy, vir_offsets[0], width_a)
    base = -(e_c[:, None, None] + e_b[None, :, None] + e_a[None, None, :]).reshape(block_c, tile)
    grad_sum = jnp.zeros((n_pair, block_c, width), jnp.float32)
    dens_list = []
    for slot in range(n_i):
        ints_full = lax.all_gather(integrals[slot], "row", axis=0, tiled=True).reshape(width, tile)
        triples = jnp.einsum("pcd,dx->pcx", amp_full, ints_full, preferred_element_type=jnp.float32)
        scaled = (triples / (occ_sum[slot][:, None, None] + base[None])).astype(jnp.bfloat16)
        z_rows = scaled.reshape(n_pair * block_c, tile)
        dens_part = lax.psum_scatter(
            lax.dot_general(
                amp_rows, z_rows, (((0,), (0,)), ((), ())), preferred_element_type=jnp.float32
            ).astype(jnp.bfloat16),
            "row",
            scatter_dimension=0,
            tiled=True,
        )
        dens_list.append(dens_part.reshape(block_d, width_b, width_a))
        grad_sum = grad_sum + jnp.einsum(
            "pcx,dx->pcd", scaled, ints_full, preferred_element_type=jnp.float32
        )
    density = jnp.stack(dens_list)
    amp_grad = lax.psum_scatter(grad_sum, "col", scatter_dimension=2, tiled=True).astype(
        jnp.bfloat16
    )
    return (density, amp_grad)


def denominators(
    i_list, pairs, vir_offsets, occ_energy, vir_smem, vir_rows, denom
):
    n_i, n_pair = i_list.shape[0], pairs.shape[0]
    block_c = denom.shape[0] // n_pair
    tile = denom.shape[1] // n_i
    width_b = tile // LANES
    row_pos = lax.axis_index("row")
    col_pos = lax.axis_index("col")
    rows_c = block_c // LANES
    e_c = vir_rows[pl.ds(row_pos * rows_c, rows_c), :]
    e_c = jnp.concatenate(
        [jnp.broadcast_to(e_c[k : k + 1, :], (LANES, LANES)).T for k in range(rows_c)], axis=0
    )
    e_a = vir_rows[pl.ds(vir_offsets[0] // LANES, 1), :]
    base = []
    for b in range(width_b):
        e_b = vir_smem[vir_offsets[1] + col_pos * width_b + b]
        base.append(-((e_c + e_b) + e_a))
    base = jnp.concatenate(base, axis=1)
    for slot in range(n_i):
        for pair in range(n_pair):
            occ = (
                occ_energy[i_list[slot]]
                + occ_energy[pairs[pair, 0]]
                + occ_energy[pairs[pair, 1]]
            )
            rows = slice(pair * block_c, (pair + 1) * block_c)
            denom[rows, slot * tile : (slot + 1) * tile] = occ + base


def first_slots(whole, part):
    part[...] = whole[: part.shape[0]]


def last_slots(whole, part):
    part[...] = whole[part.shape[0] :]


def all_rows(own, near_x, near_y, far_xy, far_yx, full):
    n_i, block_d, tile = own.shape
    half = n_i // 2
    row_pos = lax.axis_index("row")
    for mask, blocks in (
        (0, (own,)),
        (X_MASK, (near_x,)),
        (Y_MASK, (near_y,)),
        (X_MASK ^ Y_MASK, (far_xy, far_yx)),
    ):
        at = pl.multiple_of((row_pos ^ mask) * block_d, block_d)
        for slot in range(n_i):
            block = blocks[0] if slot < half else blocks[-1]
            place = slot - half if len(blocks) > 1 and slot >= half else slot
            full[pl.ds(at, block_d), slot * tile : (slot + 1) * tile] = block[place]


def products(
    denom,
    ints_full,
    ends,
    far,
    beside,
    other_ends,
    other_far,
    other_beside,
    keep_x,
    send_x,
    keep_y,
    send_y,
    grad_mine,
    grad_other,
    amp_full,
):
    n_chip, n_pair, block_c, sub_d = grad_mine.shape
    _, half, block_d, tile = keep_x.shape
    row_pos = lax.axis_index("row")
    col_pos = lax.axis_index("col")
    chip_pos = col_pos // CORES
    core_pos = col_pos % CORES
    blocks = (
        (0, ends.at[0], other_ends.at[0]),
        (1, beside, other_beside),
        (2, far, other_far),
        (3, ends.at[1], other_ends.at[1]),
    )
    for step, mine, other in blocks:
        base_d = (chip_pos ^ step) * (CORES * sub_d)
        at_mine = pl.multiple_of(base_d + core_pos * sub_d, sub_d)
        at_other = pl.multiple_of(base_d + (1 - core_pos) * sub_d, sub_d)
        for pair in range(n_pair):
            rows = slice(pair * block_c, (pair + 1) * block_c)
            amp_full[rows, pl.ds(at_mine, sub_d)] = mine[pair]
            amp_full[rows, pl.ds(at_other, sub_d)] = other[pair]

    triples = jnp.dot(amp_full[...], ints_full[...], preferred_element_type=jnp.float32)
    scaled = (triples / denom[...]).astype(jnp.bfloat16)

    low = core_pos == 0
    for step in range(n_chip):
        at = pl.multiple_of((chip_pos ^ step) * (CORES * sub_d), CORES * sub_d)
        total = lax.dot_general(
            scaled,
            ints_full[pl.ds(at, CORES * sub_d), :],
            (((1,), (1,)), ((), ())),
            preferred_element_type=jnp.float32,
        ).reshape(n_pair, block_c, CORES * sub_d)
        first, second = total[:, :, :sub_d], total[:, :, sub_d:]
        grad_mine[step] = jnp.where(low, first, second).astype(grad_mine.dtype)
        grad_other[step] = jnp.where(low, second, first).astype(grad_other.dtype)

    both = X_MASK ^ Y_MASK
    plan = (
        (0, (keep_x, 0), (keep_y, 0)),
        (X_MASK, (send_x, 0), (keep_y, 1)),
        (Y_MASK, (keep_x, 1), (send_y, 0)),
        (both, (send_x, 1), (send_y, 1)),
    )
    for mask, first, second in plan:
        at = pl.multiple_of((row_pos ^ mask) * block_d, block_d)
        total = lax.dot_general(
            amp_full[:, pl.ds(at, block_d)],
            scaled,
            (((0,), (0,)), ((), ())),
            preferred_element_type=jnp.float32,
        )
        for part_of, (out, place) in enumerate((first, second)):
            for k in range(half):
                slot = part_of * half + k
                out[place, k] = total[:, slot * tile : (slot + 1) * tile].astype(out.dtype)


def results(own_x, last_x, own_y, last_y, own, *refs):
    density, amp_grad = refs[-2:]
    total = own[...]
    for value in refs[:-2]:
        total = total + value[...].astype(jnp.float32)
    amp_grad[...] = total.astype(amp_grad.dtype)
    half = own_x.shape[0]
    for part_of, (kept, last) in enumerate(((own_x, last_x), (own_y, last_y))):
        for k in range(half):
            total = (kept[k] + last[k].astype(jnp.float32)).astype(density.dtype)
            density[part_of * half + k] = total.reshape(density.shape[1:])


def row_sums(keep, received, own, onward):
    own[...] = keep[0] + received[0].astype(jnp.float32)
    onward[...] = (keep[1] + received[1].astype(jnp.float32)).astype(onward.dtype)


def core_sums(n_chip, own, received, kept, *outs):
    kept[...] = own[0] + received[0].astype(jnp.float32)
    for step in range(1, n_chip):
        total = own[step] + received[step].astype(jnp.float32)
        outs[step - 1][...] = total.astype(outs[step - 1].dtype)


def exchanged(n_row, n_col, *args):
    i_list, pairs, vir_offsets, occ_energy, vir_energy, amplitudes, integrals = args
    n_pair, block_c, sub_d = amplitudes.shape
    n_i, block_d, width_b, width_a = integrals.shape
    width = vir_energy.shape[0]
    tile = width_b * width_a
    n_chip = n_col // CORES

    def over_row(value, mask):
        return lax.ppermute(value, "row", [(k, k ^ mask) for k in range(n_row)])

    def over_chips(value, mask):
        return lax.ppermute(value, "col", [(k, k ^ (CORES * mask)) for k in range(n_col)])

    def over_cores(value):
        return lax.ppermute(value, "col", [(k, k ^ 1) for k in range(n_col)])

    vmem = pl.BlockSpec(memory_space=pltpu.VMEM)
    smem = pl.BlockSpec(memory_space=pltpu.SMEM)
    shape = jax.ShapeDtypeStruct
    f32, bf16 = jnp.float32, jnp.bfloat16

    def room(mib):
        return pltpu.CompilerParams(vmem_limit_bytes=mib * 2**20)

    def flat(value):
        return value.reshape(value.shape[:2] + (tile,))

    half = n_i // 2

    def part_of(kernel, whole):
        return pl.pallas_call(
            kernel,
            out_shape=shape((half, block_d, tile), bf16),
            in_specs=[vmem],
            out_specs=vmem,
            compiler_params=room(4),
            name=kernel.__name__,
        )(whole)

    denom = pl.pallas_call(
        denominators,
        out_shape=shape((n_pair * block_c, n_i * tile), f32),
        in_specs=[smem] * 5 + [vmem],
        out_specs=vmem,
        compiler_params=room(4),
        name="denominators",
    )(i_list, pairs, vir_offsets, occ_energy, vir_energy, vir_energy.reshape(-1, LANES))
    across, beside, far = [over_chips(amplitudes, step) for step in (3, 1, 2)]
    ints_x, ints_y = over_row(integrals, X_MASK), over_row(integrals, Y_MASK)
    ints_own = flat(integrals)
    flat_x, flat_y = flat(ints_x), flat(ints_y)
    ints_xy = over_row(part_of(first_slots, flat_x), Y_MASK)
    ints_yx = over_row(part_of(last_slots, flat_y), X_MASK)
    across, ints_own, denom = lax.optimization_barrier((across, ints_own, denom))
    ends = jnp.stack([amplitudes, across])
    other_ends, other_far, other_beside = over_cores(ends), over_cores(far), over_cores(beside)
    ints_full = pl.pallas_call(
        all_rows,
        out_shape=shape((width, n_i * tile), bf16),
        in_specs=[vmem] * 5,
        out_specs=vmem,
        compiler_params=room(6),
        name="all_rows",
    )(ints_own, flat_x, flat_y, ints_xy, ints_yx)
    dens_shape = (2, half, block_d, tile)
    grad_shape = (n_chip, n_pair, block_c, sub_d)
    keep_x, send_x, keep_y, send_y, grad_mine, grad_other = pl.pallas_call(
        products,
        out_shape=[shape(dens_shape, f32), shape(dens_shape, bf16)] * 2
        + [shape(grad_shape, f32), shape(grad_shape, bf16)],
        in_specs=[vmem] * 8,
        out_specs=[vmem] * 6,
        scratch_shapes=[pltpu.VMEM((n_pair * block_c, width), bf16)],
        compiler_params=room(14),
        name="products",
    )(denom, ints_full, ends, far, beside, other_ends, other_far, other_beside)
    block = (n_pair, block_c, sub_d)
    grads = pl.pallas_call(
        functools.partial(core_sums, n_chip),
        out_shape=[shape(block, f32 if step == 0 else bf16) for step in range(n_chip)],
        in_specs=[vmem] * 2,
        out_specs=[vmem] * n_chip,
        compiler_params=room(6),
        name="core_sums",
    )(grad_mine, over_cores(grad_other))

    def summed(keep, received):
        return pl.pallas_call(
            row_sums,
            out_shape=[shape(dens_shape[1:], f32), shape(dens_shape[1:], bf16)],
            in_specs=[vmem] * 2,
            out_specs=[vmem] * 2,
            compiler_params=room(4),
            name="row_sums",
        )(keep, received)

    from_x, from_y = over_row(send_x, X_MASK), over_row(send_y, Y_MASK)
    near, far, across = [over_chips(grads[step], step) for step in range(1, n_chip)]
    from_x, from_y, near = lax.optimization_barrier((from_x, from_y, near))
    own_x, onward_x = summed(keep_x, from_x)
    own_y, onward_y = summed(keep_y, from_y)
    last_x, last_y = over_row(onward_x, Y_MASK), over_row(onward_y, X_MASK)
    density, amp_grad = pl.pallas_call(
        results,
        out_shape=[shape((n_i, block_d, width_b, width_a), bf16), shape(block, bf16)],
        in_specs=[vmem] * (4 + n_chip),
        out_specs=[vmem] * 2,
        compiler_params=room(6),
        name="results",
    )(own_x, last_x, own_y, last_y, grads[0], far, near, across)
    return density, amp_grad


def solution(mesh):
    n_row, n_col = mesh.shape["row"], mesh.shape["col"]

    def local(*args):
        block_c, sub_d = args[5].shape[1:]
        block_d, _, width_a = args[6].shape[1:]
        whole_tiles = (
            width_a == LANES
            and sub_d % LANES == 0
            and block_c % LANES == 0
            and block_d % LANES == 0
            and (n_row, n_col) == (4, 4 * CORES)
            and args[6].shape[0] % 2 == 0
        )
        if whole_tiles:
            return exchanged(n_row, n_col, *args)
        return gathered(*args)

    return jax.shard_map(
        local,
        mesh=mesh,
        in_specs=(P(), P(), P(), P(), P(), P(None, "row", "col"), P(None, "row", "col", None)),
        out_specs=(P(None, "row", "col", None), P(None, "row", "col")),
        check_vma=False,
    )
```
